256 devices in a mesh: dp: 16 (over z_hi, x), ctx: 16 (over z_lo, y, core).
Axes of the slice: x: 4, y: 4, z: 8 (z_hi: 4, z_lo: 2; z = z_hi * 2 + z_lo), core: 2. Of those that a mesh axis runs over, the one named last changes fastest.
Arguments:
- queries: bfloat16 [16, 2, 16, 64, 2048], P('dp', None, 'ctx'), may hold values from -24 to 24
- key_states: bfloat16 [16, 2, 16, 64, 512], P('dp', None, 'ctx'), may hold values from -24 to 24
- value_vectors: bfloat16 [16, 2, 16, 64, 512], P('dp', None, 'ctx'), may hold values from -6 to 6
- grad_out: bfloat16 [16, 2, 16, 64, 2048], P('dp', None, 'ctx'), may hold values from -6 to 6
- doc_start: int32 [16, 2, 16, 64], P('dp', None, 'ctx'), may hold values from 0 to 32767, as said below
Outputs:
- attn_out: bfloat16 [16, 2, 16, 64, 2048], P('dp', None, 'ctx')
- q_grad: bfloat16 [16, 2, 16, 64, 2048], P('dp', None, 'ctx')
- k_grad: bfloat16 [16, 2, 16, 64, 512], P('dp', None, 'ctx')
- v_grad: bfloat16 [16, 2, 16, 64, 512], P('dp', None, 'ctx')
The draws below stay inside these ranges and needn't reach their ends.
Inputs may be any that keep to these rules, and one draw needn't show every extreme that they name: Every token from doc_start of a token to that token's own position belongs to its document and carries the same doc_start; documents have at most 2048 tokens and one has exactly 2048; every document except the sequence's last token, which is a document of its own, has at least 512 tokens; a document that reaches into the positions of cycle d from an earlier cycle begins at or after position d * 2048 - 2048 // 2.
All inputs are finite; a program needn't handle non-finite values.
Results may differ from the reference program's by a relative error of at most 0.027.
Values may be sent and summed in bfloat16 or wider, within the bound.
No kernel may reach another device: no remote copies, remote signals or barrier semaphores. Data moves between devices by JAX's collectives and lax.ppermute only.
A program may use at most 128 MiB of HBM per device.

```python
import math
import jax
import jax.numpy as jnp
from jax import lax

QUERY_HEADS = 16
KEY_VALUE_HEADS = 4
HEAD_SIZE = 128
HALF_TOKENS = 64
CYCLE_COUNT = 16
CYCLE_DEVICES = 16
SPAN = 2048
ALL_TOKENS = 32768


def shared_states(key):
    base_offset = jax.random.truncated_normal(jax.random.fold_in(key, 11), -4.0, 4.0, (CYCLE_COUNT, 2, CYCLE_DEVICES, HALF_TOKENS, KEY_VALUE_HEADS * HEAD_SIZE), jnp.float32)
    return base_offset


def draw_key_states(key, part):
    base_offset = shared_states(key)
    return base_offset.astype(jnp.bfloat16)


def draw_queries(key, part):
    key = jax.random.fold_in(key, 4)
    fresh = jax.random.truncated_normal(key, -4.0, 4.0, (CYCLE_COUNT, 2, CYCLE_DEVICES, HALF_TOKENS, QUERY_HEADS * HEAD_SIZE), jnp.float32)
    return fresh.astype(jnp.bfloat16)


def draw_doc_start(key, part):
    key = jax.random.fold_in(key, 5)
    cycle_ids = jnp.arange(CYCLE_COUNT, dtype=jnp.int32)
    longest_cycle = jax.random.randint(jax.random.fold_in(key, 3), (), 1, CYCLE_COUNT, dtype=jnp.int32)
    reach_back = jax.random.randint(jax.random.fold_in(key, 1), (CYCLE_COUNT,), SPAN // 4, SPAN // 2 + 1, dtype=jnp.int32)
    reach_back = jnp.where(cycle_ids == longest_cycle, SPAN // 2, jnp.where(cycle_ids == longest_cycle + 1, SPAN // 4, reach_back)).astype(jnp.int32)
    next_back = jnp.concatenate([reach_back[1:], jnp.full((1,), SPAN // 4, jnp.int32)])
    upper = (3 * SPAN // 4 - next_back).astype(jnp.int32)
    reach_more = jax.random.randint(jax.random.fold_in(key, 2), (CYCLE_COUNT,), upper // 2, upper, dtype=jnp.int32)
    reach_more = jnp.where(cycle_ids == longest_cycle, SPAN // 2 - 1, reach_more).astype(jnp.int32)
    doc_length = reach_back + 1 + reach_more
    first_pos = cycle_ids * SPAN - reach_back
    last_pos = first_pos + doc_length
    crossing = cycle_ids >= 1
    final_cut = jnp.full((1,), ALL_TOKENS - 1, jnp.int32)
    cuts = jnp.concatenate([jnp.zeros((1,), jnp.int32), jnp.where(crossing, first_pos, 0), jnp.where(crossing & (last_pos < ALL_TOKENS), last_pos, 0), final_cut]).astype(jnp.int32)
    cycle_grid = jnp.arange(CYCLE_COUNT, dtype=jnp.int32)[:, None, None, None]
    upper_half = jnp.arange(2, dtype=jnp.int32)[None, :, None, None]
    member = jnp.arange(CYCLE_DEVICES, dtype=jnp.int32)[None, None, :, None]
    offsets = jnp.arange(HALF_TOKENS, dtype=jnp.int32)[None, None, None, :]
    block_id = jnp.where(upper_half == 0, member, 2 * CYCLE_DEVICES - 1 - member)
    positions = cycle_grid * SPAN + block_id * HALF_TOKENS + offsets
    return jnp.max(jnp.where(cuts <= positions[..., None], cuts, 0), axis=-1).astype(jnp.int32)


def steps_of(stream_key, shape, pieces, low, largest):
    def one(dim, shards_of):
        heights = jax.random.uniform(jax.random.fold_in(jax.random.fold_in(stream_key, 6), dim), (shards_of,), jnp.float32, low / len(pieces), largest / len(pieces))
        return jnp.repeat(jnp.exp(heights), shape[dim] // shards_of).reshape((-1,) + (1,) * (len(shape) - dim - 1))

    level = one(*pieces[0])
    for cut in pieces[1:]:
        level = level * one(*cut)
    return level


def bell_draw(own_key, extent, deviation, reach, pieces=(), kind=jnp.bfloat16):
    level = steps_of(own_key, extent, pieces, -0.22, 0.18) if pieces else 1.0
    values = jax.random.normal(own_key, extent, jnp.float32) * deviation * level
    return jnp.minimum(jnp.maximum(values, -reach), reach).astype(kind)


def setup_inputs(seed: int = 0) -> dict:
    streams_of = jax.random.split(jax.random.key(seed), 6)
    return {
        "queries": draw_queries(jax.random.fold_in(streams_of[5], 71), 0),
        "key_states": draw_key_states(jax.random.fold_in(streams_of[5], 71), 0),
        "value_vectors": bell_draw(streams_of[2], (CYCLE_COUNT, 2, CYCLE_DEVICES, HALF_TOKENS, KEY_VALUE_HEADS * HEAD_SIZE), 1.0, 6.0, ((0, 16), (2, 16))),
        "grad_out": bell_draw(streams_of[3], (CYCLE_COUNT, 2, CYCLE_DEVICES, HALF_TOKENS, QUERY_HEADS * HEAD_SIZE), 1.0, 6.0, ((0, 16), (2, 16))),
        "doc_start": draw_doc_start(jax.random.fold_in(streams_of[5], 71), 0),
    }


NEG_FILL = -1e30


def to_sequence(array):
    width = array.shape[-1]
    joined = jnp.concatenate([array[:, 0], array[:, 1, ::-1]], axis=1)
    return joined.reshape(array.shape[0], -1, width)


def from_sequence(array):
    width = array.shape[-1]
    blocks = array.reshape(CYCLE_COUNT, 2 * CYCLE_DEVICES, HALF_TOKENS, width)
    return jnp.stack([blocks[:, :CYCLE_DEVICES], blocks[:, CYCLE_DEVICES:][:, ::-1]], axis=1)


def block_grads(query_local_block, gradient_block, query_pos, query_start, key_gathered, value_gathered, key_pos):
    row_indices = query_local_block.shape[0]
    query_group_size = QUERY_HEADS // KEY_VALUE_HEADS
    score_scale = HEAD_SIZE ** -0.5
    query_float = query_local_block.astype(jnp.float32).reshape(row_indices, KEY_VALUE_HEADS, query_group_size, HEAD_SIZE)
    gradient_float = gradient_block.astype(jnp.float32).reshape(row_indices, KEY_VALUE_HEADS, query_group_size, HEAD_SIZE)
    key_float = key_gathered.astype(jnp.float32).reshape(-1, KEY_VALUE_HEADS, HEAD_SIZE)
    value_float = value_gathered.astype(jnp.float32).reshape(-1, KEY_VALUE_HEADS, HEAD_SIZE)
    scores = jnp.einsum('qgjd,kgd->gjqk', query_float, key_float) * score_scale
    visible = (key_pos[None, :] >= query_start[:, None]) & (key_pos[None, :] <= query_pos[:, None])
    masked = jnp.where(visible, scores, NEG_FILL)
    row_max = jnp.max(masked, axis=-1)
    lse = row_max + jnp.log(jnp.sum(jnp.exp(masked - row_max[..., None]), axis=-1))
    probs_full = jnp.where(visible, jnp.exp(scores - lse[..., None]), 0.0)
    probs = lax.optimization_barrier(probs_full.astype(jnp.bfloat16)).astype(jnp.float32)
    attn = jnp.einsum('gjqk,kgd->qgjd', probs, value_float).astype(jnp.bfloat16)
    delta = jnp.sum(attn.astype(jnp.float32) * gradient_float, axis=-1).transpose(1, 2, 0)
    dprobs = jnp.einsum('qgjd,kgd->gjqk', gradient_float, value_float)
    dscores = lax.optimization_barrier((probs_full * (dprobs - delta[..., None])).astype(jnp.bfloat16)).astype(jnp.float32)
    q_part = (jnp.einsum('gjqk,kgd->qgjd', dscores, key_float) * score_scale).astype(jnp.bfloat16)
    k_part = jnp.einsum('gjqk,qgjd->kgd', dscores, query_float) * score_scale
    v_part = jnp.einsum('gjqk,qgjd->kgd', probs, gradient_float)
    keys_count = key_float.shape[0]
    return attn.reshape(row_indices, -1), q_part.reshape(row_indices, -1), k_part.reshape(keys_count, -1), v_part.reshape(keys_count, -1)


def cycle_pass(query_cycle, grad_cycle, start_cycle, key_gathered, value_gathered, key_pos, query_pos):
    block_rows = math.gcd(SPAN, 512)
    count = SPAN // block_rows
    width_q = query_cycle.shape[-1]

    def step(carry, item):
        query_local_block, gradient_block, pos_block, start_block = item
        attn, q_part, k_part, v_part = block_grads(query_local_block, gradient_block, pos_block, start_block, key_gathered, value_gathered, key_pos)
        return (carry[0] + k_part, carry[1] + v_part), (attn, q_part)

    zero_terms = jnp.zeros(key_gathered.shape, jnp.float32)
    items = (query_cycle.reshape(count, block_rows, width_q), grad_cycle.reshape(count, block_rows, width_q),
             query_pos.reshape(count, block_rows), start_cycle.reshape(count, block_rows))
    (k_terms, v_terms), (attn, q_part) = lax.scan(step, (zero_terms, zero_terms), items)
    return attn.reshape(SPAN, width_q), q_part.reshape(SPAN, width_q), k_terms, v_terms


def reference(queries, key_states, value_vectors, grad_out, doc_start):
    query_seq = to_sequence(queries)
    key_seq = to_sequence(key_states)
    value_seq = to_sequence(value_vectors)
    grad_seq = to_sequence(grad_out)
    start_seq = to_sequence(doc_start[..., None])[..., 0].astype(jnp.int32)
    key_prev = jnp.concatenate([jnp.zeros_like(key_seq[:1]), key_seq[:-1]], axis=0)[:, SPAN // 2:]
    value_prev = jnp.concatenate([jnp.zeros_like(value_seq[:1]), value_seq[:-1]], axis=0)[:, SPAN // 2:]
    cycle_ids = jnp.arange(CYCLE_COUNT, dtype=jnp.int32)

    def one_cycle(item):
        query_cycle, grad_cycle, start_cycle, key_cycle, value_cycle, key_back, value_back, cycle_id = item
        query_pos = cycle_id * SPAN + jnp.arange(SPAN, dtype=jnp.int32)
        back_pos = (cycle_id - 1) * SPAN + SPAN // 2 + jnp.arange(SPAN // 2, dtype=jnp.int32)
        key_pos = jnp.concatenate([query_pos, back_pos]).astype(jnp.int32)
        key_gathered = jnp.concatenate([key_cycle, key_back], axis=0)
        value_gathered = jnp.concatenate([value_cycle, value_back], axis=0)
        return cycle_pass(query_cycle, grad_cycle, start_cycle, key_gathered, value_gathered, key_pos, query_pos)

    attn, q_part, k_terms, v_terms = lax.map(one_cycle, (query_seq, grad_seq, start_seq, key_seq, value_seq, key_prev, value_prev, cycle_ids))

    def settle(terms):
        own_terms = terms[:, :SPAN]
        back_terms = terms[:, SPAN:]
        carried = jnp.concatenate([back_terms[1:], jnp.zeros_like(back_terms[:1])], axis=0)
        total = own_terms + jnp.concatenate([jnp.zeros_like(carried), carried], axis=1)
        return from_sequence(total.astype(jnp.bfloat16))

    return from_sequence(attn), from_sequence(q_part), settle(k_terms), settle(v_terms)
```

```python
import jax
import jax.numpy as jnp
from jax import lax
from jax.experimental import pallas as pl
from jax.experimental.pallas import tpu as pltpu
from jax.sharding import PartitionSpec as P

HEAD = 128
HALF = 64
MEMBERS = 16
HEADS = 16
GROUPS = 4
SPAN = 2048
BACK = 1024
KEYS = SPAN + BACK
TQ = 256
TK = 512
SCALE = HEAD**-0.5
LOG2E = 1.4426950408889634
NEG = -1e30

RQ, RG, RK, RV, RPK, RPV, RS = 0, 128, 256, 384, 512, 576, 640
ROWS_IN = 656
ROWS_OUT = 640

NT = (((1,), (1,)), ((), ()))
NN = (((1,), (0,)), ((), ()))


def dot(a, b, dims=NN):
    return lax.dot_general(a, b, dims, preferred_element_type=jnp.float32)


def pack_kernel(q_ref, g_ref, k_ref, v_ref, tail_ref, s_ref, o_ref):
    for n in range(HEADS):
        g = n // (HEADS // GROUPS)
        at = slice(n * HEAD, (n + 1) * HEAD)
        kv = slice(g * HEAD, (g + 1) * HEAD)
        o_ref[n, RQ : RQ + 128] = q_ref[:, at]
        o_ref[n, RG : RG + 128] = g_ref[:, at]
        o_ref[n, RK : RK + 128] = k_ref[:, kv]
        o_ref[n, RV : RV + 128] = v_ref[:, kv]
        o_ref[n, RPK : RPK + 64] = tail_ref[0:64, kv]
        o_ref[n, RPV : RPV + 64] = tail_ref[64:128, kv]
        o_ref[n, RS : RS + 16] = s_ref[...]


def attn_kernel(r_ref, o_ref, q_s, g_s, k_s, v_s, kt_s, vt_s, st_s, p_s, dq_s, dk_s, dv_s):
    for s in range(MEMBERS):
        lo, hi = 64 * s, 64 * (31 - s)
        q_s[lo : lo + 64] = r_ref[s, RQ : RQ + 64]
        q_s[hi : hi + 64] = r_ref[s, RQ + 64 : RQ + 128]
        g_s[lo : lo + 64] = r_ref[s, RG : RG + 64]
        g_s[hi : hi + 64] = r_ref[s, RG + 64 : RG + 128]
        k_s[BACK + lo : BACK + lo + 64] = r_ref[s, RK : RK + 64]
        k_s[BACK + hi : BACK + hi + 64] = r_ref[s, RK + 64 : RK + 128]
        v_s[BACK + lo : BACK + lo + 64] = r_ref[s, RV : RV + 64]
        v_s[BACK + hi : BACK + hi + 64] = r_ref[s, RV + 64 : RV + 128]
        pv = 64 * (15 - s)
        k_s[pv : pv + 64] = r_ref[s, RPK : RPK + 64]
        v_s[pv : pv + 64] = r_ref[s, RPV : RPV + 64]
    for t in range(SPAN // 128):
        s0, s1, row = (2 * t, 2 * t + 1, 0) if t < 8 else (31 - 2 * t, 30 - 2 * t, 2)
        both = r_ref[s0, RS : RS + 16].astype(jnp.float32) + r_ref[s1, RS : RS + 16].astype(
            jnp.float32
        )
        start = both[row : row + 1] * 64.0 + both[row + 1 : row + 2]
        st_s[t // 2, 0:1, (t % 2) * 128 : (t % 2) * 128 + 128] = start.astype(jnp.int32)
    for t in range(KEYS // 256):
        at = slice(256 * t, 256 * t + 256)
        kt_s[:, at] = k_s[at].T
        vt_s[:, at] = v_s[at].T
    dk_s[...] = jnp.zeros_like(dk_s)
    dv_s[...] = jnp.zeros_like(dv_s)

    lanes = lax.broadcasted_iota(jnp.int32, (1, TQ), 1)
    rows = lax.broadcasted_iota(jnp.int32, (TK, TQ), 0)
    fold = SCALE * LOG2E

    def q_block(i, _):
        q_at = pl.ds(pl.multiple_of(i * TQ, TQ), TQ)
        qi = q_s[q_at, :]
        gi = g_s[q_at, :]
        start = st_s[i, 0:1, :]
        last = BACK + i * TQ + lanes
        first_tile = jnp.min(start) // TK
        end_tile = (BACK + i * TQ + TQ - 1) // TK + 1

        def stats(t, m8):
            at = pl.ds(pl.multiple_of(t * TK, TK), TK)
            s = dot(k_s[at, :], qi, NT)
            seen = (rows >= start - t * TK) & (rows <= last - t * TK)
            s = jnp.where(seen, s, NEG)
            p_s[at, :] = s
            return jnp.maximum(m8, jnp.max(s.reshape(TK // 8, 8, TQ), axis=0))

        m8 = lax.fori_loop(first_tile, end_tile, stats, jnp.full((8, TQ), NEG, jnp.float32))
        m = jnp.max(m8, axis=0, keepdims=True) * fold

        def outs(t, carry):
            l8, acc = carry
            at = pl.ds(pl.multiple_of(t * TK, TK), TK)
            p = jnp.exp2(p_s[at, :] * fold - m)
            p_s[at, :] = p
            l8 = l8 + jnp.sum(p.reshape(TK // 8, 8, TQ), axis=0)
            acc = acc + dot(vt_s[:, at], p.astype(jnp.bfloat16))
            return l8, acc

        l8, acc = lax.fori_loop(
            first_tile,
            end_tile,
            outs,
            (jnp.zeros((8, TQ), jnp.float32), jnp.zeros((HEAD, TQ), jnp.float32)),
        )
        inv = 1.0 / jnp.sum(l8, axis=0, keepdims=True)
        out_t = acc * inv
        delta = jnp.sum(out_t * gi.astype(jnp.float32).T, axis=0, keepdims=True)
        q_s[q_at, :] = out_t.T.astype(jnp.bfloat16)

        def grads(t, dq):
            at = pl.ds(pl.multiple_of(t * TK, TK), TK)
            p = p_s[at, :] * inv
            dp = dot(v_s[at, :], gi, NT)
            ds = (p * (dp - delta)).astype(jnp.bfloat16)
            dv_s[at, :] += dot(p.astype(jnp.bfloat16), gi)
            dk_s[at, :] += dot(ds, qi)
            return dq + dot(kt_s[:, at], ds)

        dq = lax.fori_loop(first_tile, end_tile, grads, jnp.zeros((HEAD, TQ), jnp.float32))
        dq_s[q_at, :] = (dq * SCALE).T.astype(jnp.bfloat16)
        return 0

    lax.fori_loop(0, SPAN // TQ, q_block, 0)

    for s in range(MEMBERS):
        lo, hi = 64 * s, 64 * (31 - s)
        o_ref[s, RQ : RQ + 64] = q_s[lo : lo + 64]
        o_ref[s, RQ + 64 : RQ + 128] = q_s[hi : hi + 64]
        o_ref[s, RG : RG + 64] = dq_s[lo : lo + 64]
        o_ref[s, RG + 64 : RG + 128] = dq_s[hi : hi + 64]
        for row, src, c in ((RK, dk_s, SCALE), (RV, dv_s, 1.0)):
            o_ref[s, row : row + 64] = (src[BACK + lo : BACK + lo + 64] * c).astype(jnp.bfloat16)
            o_ref[s, row + 64 : row + 128] = (src[BACK + hi : BACK + hi + 64] * c).astype(
                jnp.bfloat16
            )
        pv = 64 * (15 - s)
        o_ref[s, RPK : RPK + 64] = (dk_s[pv : pv + 64] * SCALE).astype(jnp.bfloat16)
        o_ref[s, RPV : RPV + 64] = dv_s[pv : pv + 64].astype(jnp.bfloat16)


def back_kernel(t_ref, o_ref):
    for g in range(GROUPS):
        total = t_ref[4 * g].astype(jnp.float32)
        for j in range(1, 4):
            total = total + t_ref[4 * g + j].astype(jnp.float32)
        o_ref[:, g * HEAD : (g + 1) * HEAD] = total.astype(jnp.bfloat16)


def unpack_kernel(t_ref, b_ref, a_ref, q_ref, k_ref, v_ref):
    for n in range(HEADS):
        at = slice(n * HEAD, (n + 1) * HEAD)
        a_ref[:, at] = t_ref[n, RQ : RQ + 128]
        q_ref[:, at] = t_ref[n, RG : RG + 128]
    for g in range(GROUPS):
        at = slice(g * HEAD, (g + 1) * HEAD)
        for row, back, o_ref in ((RK, 0, k_ref), (RV, 64, v_ref)):
            total = t_ref[4 * g, row : row + 128].astype(jnp.float32)
            for j in range(1, 4):
                total = total + t_ref[4 * g + j, row : row + 128].astype(jnp.float32)
            o_ref[0:64, at] = total[0:64].astype(jnp.bfloat16)
            o_ref[64:128, at] = (
                total[64:128] + b_ref[back : back + 64, at].astype(jnp.float32)
            ).astype(jnp.bfloat16)


def params(mib):
    return pltpu.CompilerParams(vmem_limit_bytes=mib * 1024 * 1024)


def on_device(queries, key_states, value_vectors, grad_out, doc_start):
    cycle = lax.axis_index("dp")
    member = lax.axis_index("ctx")
    bf = jnp.bfloat16
    q = queries.reshape(128, HEADS * HEAD)
    g = grad_out.reshape(128, HEADS * HEAD)
    k = key_states.reshape(128, GROUPS * HEAD)
    v = value_vectors.reshape(128, GROUPS * HEAD)

    tail = jnp.concatenate([k[64:], v[64:]], axis=0)
    tail = lax.ppermute(tail, "dp", [(i, i + 1) for i in range(15)])

    rel = doc_start.reshape(2, 1, HALF) - (cycle * SPAN - BACK)
    parts = jnp.concatenate([rel // 64, rel % 64], axis=1).astype(bf)
    zero = jnp.zeros_like(parts)
    first = jnp.concatenate([parts, zero], axis=2)
    second = jnp.concatenate([zero, parts], axis=2)
    even = member % 2 == 0
    starts = jnp.concatenate(
        [jnp.where(even, first[0], second[0]), jnp.where(even, second[1], first[1])], axis=0
    )
    starts = jnp.concatenate([starts, jnp.zeros((12, 128), bf)], axis=0)

    sent = pl.pallas_call(
        pack_kernel,
        out_shape=jax.ShapeDtypeStruct((HEADS, ROWS_IN, HEAD), bf),
        compiler_params=params(24),
        name="pack",
    )(q, g, k, v, tail, starts)
    got = lax.all_to_all(sent, "ctx", 0, 0, tiled=True)
    sums = pl.pallas_call(
        attn_kernel,
        out_shape=jax.ShapeDtypeStruct((MEMBERS, ROWS_OUT, HEAD), bf),
        scratch_shapes=[
            pltpu.VMEM((SPAN, HEAD), bf),
            pltpu.VMEM((SPAN, HEAD), bf),
            pltpu.VMEM((KEYS, HEAD), bf),
            pltpu.VMEM((KEYS, HEAD), bf),
            pltpu.VMEM((HEAD, KEYS), bf),
            pltpu.VMEM((HEAD, KEYS), bf),
            pltpu.VMEM((SPAN // TQ, 8, TQ), jnp.int32),
            pltpu.VMEM((KEYS, TQ), jnp.float32),
            pltpu.VMEM((SPAN, HEAD), bf),
            pltpu.VMEM((KEYS, HEAD), jnp.float32),
            pltpu.VMEM((KEYS, HEAD), jnp.float32),
        ],
        compiler_params=params(48),
        name="attention",
    )(got)
    home = lax.all_to_all(sums, "ctx", 0, 0, tiled=True)
    back = pl.pallas_call(
        back_kernel,
        out_shape=jax.ShapeDtypeStruct((128, GROUPS * HEAD), bf),
        compiler_params=params(24),
        name="back",
    )(home[:, RPK:])
    back = lax.ppermute(back, "dp", [(i + 1, i) for i in range(15)])
    attn, q_grad, k_grad, v_grad = pl.pallas_call(
        unpack_kernel,
        out_shape=[
            jax.ShapeDtypeStruct(q.shape, bf),
            jax.ShapeDtypeStruct(q.shape, bf),
            jax.ShapeDtypeStruct(k.shape, bf),
            jax.ShapeDtypeStruct(k.shape, bf),
        ],
        compiler_params=params(24),
        name="unpack",
    )(home, back)
    return (
        attn.reshape(queries.shape),
        q_grad.reshape(queries.shape),
        k_grad.reshape(key_states.shape),
        v_grad.reshape(value_vectors.shape),
    )


def solution(mesh):
    wide = P("dp", None, "ctx", None, None)
    return jax.shard_map(
        on_device,
        mesh=mesh,
        in_specs=(wide, wide, wide, wide, P("dp", None, "ctx", None)),
        out_specs=(wide, wide, wide, wide),
        check_vma=False,
    )
```

```python
import jax
import jax.numpy as jnp
from jax import lax
from jax.experimental import pallas as pl
from jax.experimental.pallas import tpu as pltpu
from jax.sharding import PartitionSpec as P

HEAD = 128
HALF = 64
MEMBERS = 16
HEADS = 16
GROUPS = 4
SPAN = 2048
BACK = 1024
TQ = 512
TK = 256
QB = SPAN // TQ
QS = TQ // HALF
KS = TK // HALF
OWN_TILES = SPAN // TK
BACK_TILES = BACK // TK
SCALE = HEAD**-0.5
FOLD = SCALE * 1.4426950408889634
NEG = -1e30
BF = jnp.bfloat16
F32 = jnp.float32

IN_Q, IN_G, IN_X, IN_S, IN_ROWS = 0, 128, 256, 384, 400
OUT_A, OUT_Q, OUT_X, OUT_ROWS = 0, 128, 256, 384

NT = (((1,), (1,)), ((), ()))
NN = (((1,), (0,)), ((), ()))


def dot(a, b, dims=NN):
    return lax.dot_general(a, b, dims, preferred_element_type=F32)


def begin(pairs, sems):
    copies = [pltpu.make_async_copy(a, b, sems.at[i]) for i, (a, b) in enumerate(pairs)]
    for c in copies:
        c.start()
    return copies


def finish(copies):
    for c in copies:
        c.wait()


def columns(n):
    return pl.ds(n * HEAD, HEAD)


def halves(ref, row, to, at=0):
    return [
        (ref.at[:, pl.ds(row, HALF)], to.at[pl.ds(at, MEMBERS)]),
        (ref.at[:, pl.ds(row + HALF, HALF)], to.at[pl.ds(at + MEMBERS, MEMBERS)]),
    ]


def pack_kernel(q_ref, g_ref, k_ref, v_ref, s_ref, o_ref, sems):
    pairs = []
    for n in range(HEADS):
        x_ref = k_ref if n % 2 == 0 else v_ref
        pairs.append((q_ref.at[:, columns(n)], o_ref.at[n, pl.ds(IN_Q, 128)]))
        pairs.append((g_ref.at[:, columns(n)], o_ref.at[n, pl.ds(IN_G, 128)]))
        pairs.append((x_ref.at[:, columns(n // 4)], o_ref.at[n, pl.ds(IN_X, 128)]))
    copies = begin(pairs, sems)
    for n in range(HEADS):
        o_ref[n, IN_S : IN_S + 16] = s_ref[...]
    finish(copies)


def block_of(i, st_ref):
    start = st_ref[i]
    lane = lax.broadcasted_iota(jnp.int32, (1, TQ), 1)
    part = lane // HALF
    upper = i >= QB // 2
    source = (i - QB // 2) * QS + part
    block = jnp.where(upper, 2 * MEMBERS - 1 - source, i * QS + part)
    last = BACK + block * HALF + lane % HALF
    return start, last, jnp.min(start) // TK, jnp.max(last) // TK + 1


def masked(s, start, last, base, turned, fill=NEG):
    rows = lax.broadcasted_iota(jnp.int32, (HALF, TQ), 0)
    parts = []
    for b in range(KS):
        off = base + HALF * jnp.where(turned, KS - 1 - b, b)
        seen = (rows >= start - off) & (rows <= last - off)
        parts.append(jnp.where(seen, s[b * HALF : (b + 1) * HALF], fill))
    return jnp.concatenate(parts, axis=0)


def own_tile(t):
    u = t - BACK_TILES
    turned = u >= OWN_TILES // 2
    return jnp.where(turned, OWN_TILES + OWN_TILES // 2 - 1 - u, u), turned


def back_tile(t):
    return BACK_TILES - 1 - t, True


def rows_of(ref, at, count):
    return ref[pl.ds(at * count, count)].reshape(count * HALF, HEAD)


def softmax_tiles(lo, hi, place, qi, start, last, k_at, vt_s, carry):
    def tile(t, carry):
        m, l8, acc = carry
        at, turned = place(t)
        s = dot(k_at(at), qi, NT) * FOLD
        s = masked(s, start, last, t * TK, turned)
        m_new = jnp.maximum(m, jnp.max(s, axis=0, keepdims=True))
        p = jnp.exp2(s - m_new)
        keep = jnp.exp2(m - m_new)
        l8 = l8 * keep + jnp.sum(p.reshape(TK // 8, 8, TQ), axis=0)
        acc = acc * keep + dot(vt_s[at], p.astype(BF))
        return m_new, l8, acc

    return lax.fori_loop(lo, hi, tile, carry)


def grad_tiles(lo, hi, place, qi, gi, start, last, lse, delta, k_at, v_at, kt_s, dk_s, dv_s, dq):
    def tile(t, dq):
        at, turned = place(t)
        s = masked(dot(k_at(at), qi, NT) * FOLD - lse, start, last, t * TK, turned)
        p = jnp.exp2(s)
        dp = dot(v_at(at), gi, NT)
        ds = (p * (dp - delta)).astype(BF)
        dv_s[at] += dot(p.astype(BF), gi)
        dk_s[at] += dot(ds, qi)
        return dq + dot(kt_s[at], ds)

    return lax.fori_loop(lo, hi, tile, dq)


def forward_own_kernel(core_ref, a_ref, x_ref, st_ref, m_ref, l_ref, acc_ref, q_s, kv_s, s_s, vt_s, acc_s, sems):
    core = core_ref[0]
    copies = begin(
        halves(a_ref, IN_X, kv_s.at[core])
        + halves(x_ref, 0, kv_s.at[1 - core])
        + [(a_ref.at[:, pl.ds(IN_S, 16)], s_s)]
        + halves(a_ref, IN_Q, q_s),
        sems,
    )
    finish(copies[:5])
    for t in range(SPAN // 128):
        s0, row = (2 * t, 0) if t < 8 else (2 * t - 16, 2)
        both = s_s[s0].astype(F32) + s_s[s0 + 1].astype(F32)
        start = both[row : row + 1] * 64.0 + both[row + 1 : row + 2]
        c = (t % 4) * 128
        st_ref[t // 4, 0:1, c : c + 128] = start.astype(jnp.int32)
    for t in range(OWN_TILES):
        vt_s[t] = rows_of(kv_s.at[1], t, KS).T
    finish(copies[5:])

    def q_block(i, _):
        qi = rows_of(q_s, i, QS)
        start, last, first, end = block_of(i, st_ref)
        m, l8, acc = softmax_tiles(
            jnp.maximum(first, BACK_TILES),
            end,
            own_tile,
            qi,
            start,
            last,
            lambda at: rows_of(kv_s.at[0], at, KS),
            vt_s,
            (jnp.full((1, TQ), NEG, F32), jnp.zeros((8, TQ), F32), jnp.zeros((HEAD, TQ), F32)),
        )
        m_ref[i] = m
        l_ref[i] = jnp.sum(l8, axis=0, keepdims=True)
        acc_s[i] = acc
        pltpu.make_async_copy(acc_s.at[i], acc_ref.at[i], sems.at[7 + i]).start()
        return 0

    lax.fori_loop(0, QB, q_block, 0)
    for i in range(QB):
        pltpu.make_async_copy(acc_s.at[i], acc_ref.at[i], sems.at[7 + i]).wait()


def back_kernel(
    core_ref, a_ref, p_ref, x_ref, st_ref, m_ref, l_ref, acc_ref,
    lse_ref, delta_ref, out_ref, dq_ref, keep_ref, give_ref,
    q_s, g_s, kv_s, vt_s, kt_s, acc_s, dq_s, o_s, dk_s, dv_s, sems,
):
    core = core_ref[0]
    copies = begin(
        [(p_ref, kv_s.at[core]), (x_ref, kv_s.at[1 - core])]
        + halves(a_ref, IN_Q, q_s)
        + halves(a_ref, IN_G, g_s)
        + [(acc_ref, acc_s)],
        sems,
    )
    finish(copies[:2])
    for t in range(BACK_TILES):
        kt_s[t] = rows_of(kv_s.at[0], t, KS).T
        vt_s[t] = rows_of(kv_s.at[1], t, KS).T
    dk_s[...] = jnp.zeros_like(dk_s)
    dv_s[...] = jnp.zeros_like(dv_s)
    finish(copies[2:])

    def outs(i):
        at, row = i // 2, i % 2
        return pltpu.make_async_copy(
            o_s.at[pl.ds(i * QS, QS)],
            out_ref.at[pl.ds((i % 2) * QS, QS), pl.ds(pl.multiple_of(OUT_A + (i // 2) * HALF, HALF), HALF)],
            sems.at[7 + i],
        )

    def dqs(i):
        return pltpu.make_async_copy(dq_s.at[i], dq_ref.at[i], sems.at[11 + i])

    def q_block(i, _):
        qi = rows_of(q_s, i, QS)
        gi = rows_of(g_s, i, QS)
        start, last, first, end = block_of(i, st_ref)
        l8 = jnp.concatenate([l_ref[i], jnp.zeros((7, TQ), F32)], axis=0)
        m, l8, acc = softmax_tiles(
            first,
            BACK_TILES,
            back_tile,
            qi,
            start,
            last,
            lambda at: rows_of(kv_s.at[0], at, KS),
            vt_s,
            (m_ref[i], l8, acc_s[i]),
        )
        l = jnp.sum(l8, axis=0, keepdims=True)
        out_t = acc * (1.0 / l)
        lse = m + jnp.log2(l)
        lse_ref[i] = lse
        delta = jnp.sum(out_t * gi.astype(F32).T, axis=0, keepdims=True)
        delta_ref[i] = delta
        o_s[pl.ds(i * QS, QS)] = out_t.T.astype(BF).reshape(QS, HALF, HEAD)
        outs(i).start()
        dq_s[i] = grad_tiles(
            first,
            BACK_TILES,
            back_tile,
            qi,
            gi,
            start,
            last,
            lse,
            delta,
            lambda at: rows_of(kv_s.at[0], at, KS),
            lambda at: rows_of(kv_s.at[1], at, KS),
            kt_s,
            dk_s,
            dv_s,
            jnp.zeros((HEAD, TQ), F32),
        )
        dqs(i).start()
        return 0

    lax.fori_loop(0, QB, q_block, 0)
    even = core == 0
    for t in range(BACK_TILES):
        dk, dv = dk_s[t] * SCALE, dv_s[t]
        at = slice(t * KS, (t + 1) * KS)
        keep_ref[at] = jnp.where(even, dk, dv).astype(BF).reshape(KS, HALF, HEAD)
        give_ref[at] = jnp.where(even, dv, dk).astype(BF).reshape(KS, HALF, HEAD)
    for i in range(QB):
        outs(i).wait()
        dqs(i).wait()


def own_kernel(
    core_ref, a_ref, x_ref, st_ref, lse_ref, delta_ref, dq_ref, old_ref, after_ref,
    out_ref, keep_ref, give_ref,
    q_s, g_s, kv_s, kt_s, dq_s, o_s, dk_s, dv_s, sems,
):
    core = core_ref[0]
    copies = begin(
        halves(a_ref, IN_X, kv_s.at[core])
        + halves(x_ref, 0, kv_s.at[1 - core])
        + halves(a_ref, IN_Q, q_s)
        + halves(a_ref, IN_G, g_s)
        + [(dq_ref, dq_s)],
        sems,
    )
    dk_s[...] = jnp.zeros_like(dk_s)
    dv_s[...] = jnp.zeros_like(dv_s)
    finish(copies[:4])
    for t in range(OWN_TILES):
        kt_s[t] = rows_of(kv_s.at[0], t, KS).T
    finish(copies[4:])

    def outs(i):
        return pltpu.make_async_copy(
            o_s.at[pl.ds(i * QS, QS)],
            out_ref.at[pl.ds((i % 2) * QS, QS), pl.ds(pl.multiple_of(OUT_Q + (i // 2) * HALF, HALF), HALF)],
            sems.at[9 + i],
        )

    def q_block(i, _):
        qi = rows_of(q_s, i, QS)
        gi = rows_of(g_s, i, QS)
        start, last, first, end = block_of(i, st_ref)
        dq = grad_tiles(
            jnp.maximum(first, BACK_TILES),
            end,
            own_tile,
            qi,
            gi,
            start,
            last,
            lse_ref[i],
            delta_ref[i],
            lambda at: rows_of(kv_s.at[0], at, KS),
            lambda at: rows_of(kv_s.at[1], at, KS),
            kt_s,
            dk_s,
            dv_s,
            dq_s[i],
        )
        o_s[pl.ds(i * QS, QS)] = (dq * SCALE).T.astype(BF).reshape(QS, HALF, HEAD)
        outs(i).start()
        return 0

    lax.fori_loop(0, QB, q_block, 0)
    even = core == 0
    for t in range(OWN_TILES):
        dk, dv = dk_s[t] * SCALE, dv_s[t]
        half, s0 = t // (OWN_TILES // 2), (t % (OWN_TILES // 2)) * KS
        at = (slice(s0, s0 + KS), slice(half * HALF, half * HALF + HALF))
        keep_ref[at] = jnp.where(even, dk, dv).astype(BF).reshape(KS, HALF, HEAD)
        give_ref[at] = jnp.where(even, dv, dk).astype(BF).reshape(KS, HALF, HEAD)
    for i in range(QB):
        outs(i).wait()


def tie_kernel(x_ref, after_ref, o_ref, sems):
    del x_ref, after_ref, o_ref, sems


def merge_kernel(keep_ref, got_ref, back_ref, old_ref, out_ref, x_s, sems):
    lower, upper = slice(0, HALF), slice(HALF, 2 * HALF)
    x_s[:, lower] = (keep_ref[:, lower].astype(F32) + got_ref[:, lower].astype(F32)).astype(BF)
    total = keep_ref[:, upper].astype(F32) + got_ref[:, upper].astype(F32)
    x_s[:, upper] = (total + back_ref[...].astype(F32)).astype(BF)
    finish(begin([(x_s, out_ref.at[:, pl.ds(OUT_X, 128)])], sems))


def unpack_kernel(t_ref, a_ref, q_ref, k_ref, v_ref, sems):
    pairs = []
    for n in range(HEADS):
        pairs.append((t_ref.at[n, pl.ds(OUT_A, 128)], a_ref.at[:, columns(n)]))
        pairs.append((t_ref.at[n, pl.ds(OUT_Q, 128)], q_ref.at[:, columns(n)]))
    copies = begin(pairs, sems)
    for g in range(GROUPS):
        at = slice(g * HEAD, (g + 1) * HEAD)
        for n, o_ref in ((4 * g, k_ref), (4 * g + 1, v_ref)):
            total = t_ref[n, OUT_X : OUT_X + 128].astype(F32) + t_ref[
                n + 2, OUT_X : OUT_X + 128
            ].astype(F32)
            o_ref[:, at] = total.astype(BF)
    finish(copies)


def shape(dims, dtype=BF):
    return jax.ShapeDtypeStruct(dims, dtype)


HBM = pl.BlockSpec(memory_space=pltpu.HBM)
VMEM = pl.BlockSpec(memory_space=pltpu.VMEM)
SMEM = pl.BlockSpec(memory_space=pltpu.SMEM)


def call(kernel, name, us, ins, outs, scratch, copies, mib=32, **more):
    return pl.pallas_call(
        kernel,
        in_specs=ins,
        out_specs=[space for space, _ in outs],
        out_shape=[what for _, what in outs],
        scratch_shapes=scratch + [pltpu.SemaphoreType.DMA((copies,))],
        compiler_params=pltpu.CompilerParams(vmem_limit_bytes=mib * 1024 * 1024),
        cost_estimate=pl.CostEstimate(
            flops=int(us * 4e8), bytes_accessed=1 << 20, transcendentals=0
        ),
        name=name,
        **more,
    )


def tie(x, after):
    (x,) = call(
        tie_kernel,
        "tie",
        1,
        [HBM, HBM],
        [(HBM, shape(x.shape))],
        [],
        1,
        input_output_aliases={0: 0},
    )(x, after)
    return x


def on_device(queries, key_states, value_vectors, grad_out, doc_start):
    cycle = lax.axis_index("dp")
    core = lax.axis_index("ctx") % 2
    q = queries.reshape(128, HEADS * HEAD)
    g = grad_out.reshape(128, HEADS * HEAD)
    k = key_states.reshape(128, GROUPS * HEAD)
    v = value_vectors.reshape(128, GROUPS * HEAD)
    swap = [(i, i ^ 1) for i in range(MEMBERS)]
    which = core.reshape(1)

    rel = doc_start.reshape(2, HALF) - (cycle * SPAN - BACK)
    parts = jnp.stack([rel // 64, rel % 64], axis=1).reshape(4, HALF).astype(BF)
    zero = jnp.zeros_like(parts)
    starts = jnp.where(
        core == 0,
        jnp.concatenate([parts, zero], axis=1),
        jnp.concatenate([zero, parts], axis=1),
    )
    starts = jnp.pad(starts, ((0, 12), (0, 0)))

    rows = pltpu.VMEM((2 * MEMBERS, HALF, HEAD), BF)
    own_kv = pltpu.VMEM((2, 2 * MEMBERS, HALF, HEAD), BF)
    back_kv = pltpu.VMEM((2, MEMBERS, HALF, HEAD), BF)
    wide = pltpu.VMEM((QB, HEAD, TQ), F32)
    line = (VMEM, shape((QB, 1, TQ), F32))

    def turned(tiles):
        return pltpu.VMEM((tiles, HEAD, TK), BF)

    def sums(tiles):
        return pltpu.VMEM((tiles, TK, HEAD), F32)

    (a,) = call(
        pack_kernel,
        "pack",
        1,
        [HBM, HBM, HBM, HBM, VMEM],
        [(VMEM, shape((HEADS, IN_ROWS, HEAD)))],
        [],
        3 * HEADS,
    )(*(pltpu.with_memory_space_constraint(each, pltpu.HBM) for each in (q, g, k, v)), starts)
    a = lax.all_to_all(a, "ctx", 0, 0, tiled=True)
    x = lax.ppermute(a[:, IN_X : IN_X + 128], "ctx", swap)
    p = lax.ppermute(a[:, IN_X + HALF : IN_X + 128], "dp", [(i, i + 1) for i in range(15)])
    st, m, l, acc = call(
        forward_own_kernel,
        "forward_own",
        9,
        [SMEM, HBM, HBM],
        [(VMEM, shape((QB, 1, TQ), jnp.int32)), line, line, (HBM, shape((QB, HEAD, TQ), F32))],
        [rows, own_kv, pltpu.VMEM((MEMBERS, 16, HEAD), BF), turned(OWN_TILES), wide],
        7 + QB,
    )(which, a, x)
    p = tie(p, m)
    px = lax.ppermute(p, "ctx", swap)
    lse, delta, out, dq, keep_back, give_back = call(
        back_kernel,
        "back",
        7,
        [SMEM, HBM, HBM, HBM, VMEM, VMEM, VMEM, HBM],
        [
            line,
            line,
            (HBM, shape((MEMBERS, OUT_ROWS, HEAD))),
            (HBM, shape((QB, HEAD, TQ), F32)),
            (VMEM, shape((MEMBERS, HALF, HEAD))),
            (VMEM, shape((MEMBERS, HALF, HEAD))),
        ],
        [rows, rows, back_kv, turned(BACK_TILES), turned(BACK_TILES), wide, wide, rows]
        + [sums(BACK_TILES), sums(BACK_TILES)],
        7 + 2 * QB,
    )(which, a, p, px, st, m, l, acc)
    got_back = lax.ppermute(give_back, "ctx", swap)
    back = (keep_back.astype(F32) + got_back.astype(F32)).astype(BF)
    sent_back = lax.ppermute(back, "dp", [(i + 1, i) for i in range(15)])
    out, keep, give = call(
        own_kernel,
        "own",
        11,
        [SMEM, HBM, HBM, VMEM, VMEM, VMEM, HBM, HBM, HBM],
        [
            (HBM, shape((MEMBERS, OUT_ROWS, HEAD))),
            (VMEM, shape((MEMBERS, 128, HEAD))),
            (VMEM, shape((MEMBERS, 128, HEAD))),
        ],
        [rows, rows, own_kv, turned(OWN_TILES), wide, rows, sums(OWN_TILES), sums(OWN_TILES)],
        9 + QB,
        input_output_aliases={7: 0},
    )(which, a, x, st, lse, delta, dq, out, back)
    got = lax.ppermute(tie(give, sent_back), "ctx", swap)
    (out,) = call(
        merge_kernel,
        "merge",
        1,
        [VMEM, VMEM, VMEM, HBM],
        [(HBM, shape((MEMBERS, OUT_ROWS, HEAD)))],
        [pltpu.VMEM((MEMBERS, 128, HEAD), BF)],
        1,
        input_output_aliases={3: 0},
    )(keep, got, sent_back, out)
    out = lax.all_to_all(out, "ctx", 0, 0, tiled=True)
    attn, q_grad, k_grad, v_grad = call(
        unpack_kernel,
        "unpack",
        2,
        [VMEM],
        [(HBM, shape(q.shape)), (HBM, shape(q.shape)), (VMEM, shape(k.shape)), (VMEM, shape(k.shape))],
        [],
        2 * HEADS,
    )(out)
    return (
        attn.reshape(queries.shape),
        q_grad.reshape(queries.shape),
        k_grad.reshape(key_states.shape),
        v_grad.reshape(value_vectors.shape),
    )


def solution(mesh):
    wide = P("dp", None, "ctx", None, None)
    return jax.shard_map(
        on_device,
        mesh=mesh,
        in_specs=(wide, wide, wide, wide, P("dp", None, "ctx", None)),
        out_specs=(wide, wide, wide, wide),
        check_vma=False,
    )
```

```python
from functools import partial

import jax
import jax.numpy as jnp
from jax import lax
from jax.experimental import pallas as pl
from jax.experimental.pallas import tpu as pltpu
from jax.sharding import PartitionSpec as P

HEAD = 128
HALF = 64
MEMBERS = 16
HEADS = 16
GROUPS = 4
SPAN = 2048
BACK = 1024
TQ = 512
TK = 512
QB = SPAN // TQ
QS = TQ // HALF
KS = TK // HALF
OWN_TILES = SPAN // TK
BACK_TILES = BACK // TK
SCALE = HEAD**-0.5
FOLD = SCALE * 1.4426950408889634
NEG = -1e30
BF = jnp.bfloat16
F32 = jnp.float32

IN_Q, IN_G, IN_X, IN_S, IN_ROWS = 0, 128, 256, 448, 464
OUT_A, OUT_Q, OUT_X, OUT_ROWS = 0, 128, 256, 384

NT = (((1,), (1,)), ((), ()))
NN = (((1,), (0,)), ((), ()))


def dot(a, b, dims=NN):
    return lax.dot_general(a, b, dims, preferred_element_type=F32)


def begin(pairs, sems):
    copies = [pltpu.make_async_copy(a, b, sems.at[i]) for i, (a, b) in enumerate(pairs)]
    for c in copies:
        c.start()
    return copies


def finish(copies):
    for c in copies:
        c.wait()


def columns(n):
    return pl.ds(n * HEAD, HEAD)


def pack_kernel(q_ref, g_ref, k_ref, v_ref, o_ref, sems):
    pairs = []
    for n in range(HEADS):
        x_ref = k_ref if n % 2 == 0 else v_ref
        pairs.append((q_ref.at[:, columns(n)], o_ref.at[n, pl.ds(IN_Q, 128)]))
        pairs.append((g_ref.at[:, columns(n)], o_ref.at[n, pl.ds(IN_G, 128)]))
        pairs.append((x_ref.at[:, columns(n // 4)], o_ref.at[n, pl.ds(IN_X, 128)]))
    finish(begin(pairs, sems))


def pack_tail_kernel(tail_ref, s_ref, old_ref, o_ref, x_s, sems):
    del old_ref
    for n in range(HEADS):
        row = (n % 2) * HALF
        x_s[n, 0:HALF] = tail_ref[row : row + HALF, n // 4 * HEAD : (n // 4 + 1) * HEAD]
        x_s[n, HALF : HALF + 16] = s_ref[...]
    finish(begin([(x_s, o_ref.at[:, pl.ds(IN_X + 128, HALF + 16)])], sems))


def low_position(i):
    source = (i - QB // 2) * QS + QS - 1
    upper = (2 * MEMBERS - 1 - source) * HALF
    return BACK + jnp.where(i >= QB // 2, upper, i * TQ)


def block_of(i, st_ref, plan_ref):
    lane = lax.broadcasted_iota(jnp.int32, (1, TQ), 1)
    part = lane // HALF
    part = jnp.where(i >= QB // 2, QS - 1 - part, part)
    low = low_position(i)
    end = (low + TQ - 1) // TK + 1
    whole = (plan_ref[2 * QB + i], low)
    return st_ref[i], low + part * HALF + lane % HALF, plan_ref[QB + i], end, whole


def masked(s, start, last, base, turned, fill=NEG):
    rows = lax.broadcasted_iota(jnp.int32, (HALF, TQ), 0)
    parts = []
    for b in range(KS):
        off = base + HALF * jnp.where(turned, KS - 1 - b, b)
        seen = (rows >= start - off) & (rows <= last - off)
        parts.append(jnp.where(seen, s[b * HALF : (b + 1) * HALF], fill))
    return jnp.concatenate(parts, axis=0)


def place(t):
    upper = t >= BACK_TILES + OWN_TILES // 2
    turned = (t < BACK_TILES) | upper
    top = jnp.where(upper, 2 * BACK_TILES + OWN_TILES + OWN_TILES // 2 - 1, BACK_TILES - 1)
    return jnp.where(turned, top - t, t), turned


def packet_rows(ref, i, row):
    half = pl.ds(pl.multiple_of(row + (i // 2) * HALF, HALF), HALF)
    return ref[pl.ds((i % 2) * QS, QS), half].reshape(TQ, HEAD)


def rows_of(ref, at, count):
    return ref[pl.ds(at * count, count)].reshape(count * HALF, HEAD)


def inside(whole, t):
    return (t * TK >= whole[0]) & (t * TK + TK - 1 <= whole[1])


def softmax_tiles(lo, hi, qi, start, last, clear, kv_s, vt_s, acc_s):
    acc_s[...] = jnp.zeros_like(acc_s)

    def tile(whole, t, m, l8):
        at, turned = place(t)
        s = dot(rows_of(kv_s.at[0], at, KS), qi, NT) * FOLD
        if not whole:
            s = masked(s, start, last, t * TK, turned)
        m_new = jnp.maximum(m, jnp.max(s, axis=0, keepdims=True))
        p = jnp.exp2(s - m_new)
        keep = jnp.exp2(m - m_new)
        l8 = l8 * keep + jnp.sum(p.reshape(TK // 8, 8, TQ), axis=0)
        acc_s[...] = acc_s[...] * keep + dot(vt_s[at], p.astype(BF))
        return m_new, l8

    def either(t, carry):
        return lax.cond(
            inside(clear, t), partial(tile, True), partial(tile, False), t, *carry
        )

    return lax.fori_loop(
        lo, hi, either, (jnp.full((1, TQ), NEG, F32), jnp.zeros((8, TQ), F32))
    )


def grad_tiles(lo, hi, base, qi, gi, start, last, clear, lse, delta, kv_s, kt_s, dk_s, dv_s, dq_s):
    def tile(whole, t):
        at, turned = place(t)
        s = dot(rows_of(kv_s.at[0], at, KS), qi, NT) * FOLD - lse
        if not whole:
            s = masked(s, start, last, t * TK, turned)
        p = jnp.exp2(s)
        dp = dot(rows_of(kv_s.at[1], at, KS), gi, NT)
        at = at - base
        ds = (p * (dp - delta)).astype(BF)
        dv_s[at] += dot(p.astype(BF), gi)
        dk_s[at] += dot(ds, qi)
        dq_s[...] += dot(kt_s[at], ds)
        return 0

    def either(t, _):
        return lax.cond(inside(clear, t), partial(tile, True), partial(tile, False), t)

    lax.fori_loop(lo, hi, either, 0)


def forward_block(i, qi, gi, start, last, clear, first, end, kv_s, vt_s, acc_s, o_s):
    m, l8 = softmax_tiles(first, end, qi, start, last, clear, kv_s, vt_s, acc_s)
    l = jnp.sum(l8, axis=0, keepdims=True)
    out_t = acc_s[...] * (1.0 / l)
    delta = jnp.sum(out_t * gi.astype(F32).T, axis=0, keepdims=True)
    o_s[pl.ds(i * QS, QS)] = out_t.T.astype(BF).reshape(QS, HALF, HEAD)
    return m + jnp.log2(l), delta


def block_out(i, row, o_s, out_ref, sem):
    half = pl.ds(pl.multiple_of(row + (i // 2) * HALF, HALF), HALF)
    return pltpu.make_async_copy(
        o_s.at[pl.ds(i * QS, QS)], out_ref.at[pl.ds((i % 2) * QS, QS), half], sem
    )


def forward_kernel(
    core_ref, a_ref, x_ref,
    st_ref, kv_s, lse_ref, delta_ref, out_ref, dq_ref, keep_ref, give_ref, plan_ref,
    vt_s, kt_s, acc_s, o_s, dk_s, dv_s, sems,
):
    core = core_ref[0]
    for part, row in enumerate((128, 0, HALF)):
        at = slice(part * MEMBERS, (part + 1) * MEMBERS)
        mine = a_ref[:, IN_X + row : IN_X + row + HALF]
        theirs = x_ref[:, row : row + HALF]
        kv_s[0, at] = jnp.where(core == 0, mine, theirs)
        kv_s[1, at] = jnp.where(core == 0, theirs, mine)
    for t in range(SPAN // 128):
        s0, row = (2 * t, 0) if t < 8 else (2 * t - 16, 2)
        both = a_ref[s0, IN_S : IN_S + 16].astype(F32) + a_ref[s0 + 1, IN_S : IN_S + 16].astype(F32)
        start = both[row : row + 1] * 64.0 + both[row + 1 : row + 2]
        c = (t % 4) * 128
        st_ref[t // 4, 0:1, c : c + 128] = start.astype(jnp.int32)
    for t in range(BACK_TILES + OWN_TILES):
        vt_s[t] = rows_of(kv_s.at[1], t, KS).T
    for t in range(BACK_TILES):
        kt_s[t] = rows_of(kv_s.at[0], t, KS).T
    dk_s[...] = jnp.zeros_like(dk_s)
    dv_s[...] = jnp.zeros_like(dv_s)

    spans = []
    for i in range(QB):
        first = jnp.min(st_ref[i]) // TK
        plan_ref[QB + i] = first
        plan_ref[2 * QB + i] = jnp.max(st_ref[i])
        spans.append((first, (low_position(i) + TQ - 1) // TK + 1))
    budget = core_ref[1]
    for first, end in spans:
        reach = jnp.maximum(BACK_TILES - first, 0)
        budget -= jnp.where(reach > 0, 4 * (end - first) + 5 * reach + 2, 0)
    for i, (first, end) in enumerate(spans):
        need = 4 * (end - first) + 2
        extra = (first >= BACK_TILES) & (need <= budget)
        budget -= jnp.where(extra, need, 0)
        plan_ref[i] = ((first < BACK_TILES) | extra).astype(jnp.int32)

    def q_block(i, _):
        @pl.when(plan_ref[i] == 1)
        def _():
            start, last, first, end, clear = block_of(i, st_ref, plan_ref)
            qi = packet_rows(a_ref, i, IN_Q)
            gi = packet_rows(a_ref, i, IN_G)
            lse, delta = forward_block(i, qi, gi, start, last, clear, first, end, kv_s, vt_s, acc_s, o_s)
            lse_ref[i] = lse
            delta_ref[i] = delta
            out = block_out(i, OUT_A, o_s, out_ref, sems.at[0])
            out.start()
            dq_ref[i] = jnp.zeros((HEAD, TQ), F32)
            grad_tiles(
                first,
                BACK_TILES,
                0,
                qi,
                gi,
                start,
                last,
                clear,
                lse,
                delta,
                kv_s,
                kt_s,
                dk_s,
                dv_s,
                dq_ref.at[i],
            )
            out.wait()

        return 0

    lax.fori_loop(0, QB, q_block, 0)
    even = core == 0
    for t in range(BACK_TILES):
        dk, dv = dk_s[t] * SCALE, dv_s[t]
        at = slice(t * KS, (t + 1) * KS)
        keep_ref[at] = jnp.where(even, dk, dv).astype(BF).reshape(KS, HALF, HEAD)
        give_ref[at] = jnp.where(even, dv, dk).astype(BF).reshape(KS, HALF, HEAD)


def own_kernel(
    core_ref, plan_ref, a_ref, kv_ref, st_ref, lse_ref, delta_ref, dq_ref, old_ref, after_ref,
    out_ref, keep_ref, give_ref,
    vt_s, kt_s, lse_s, delta_s, dq_s, a_s, o_s, dk_s, dv_s, sems,
):
    del old_ref, after_ref
    core = core_ref[0]
    dk_s[...] = jnp.zeros_like(dk_s)
    dv_s[...] = jnp.zeros_like(dv_s)
    for t in range(OWN_TILES):
        kt_s[t] = rows_of(kv_ref.at[0], BACK_TILES + t, KS).T
        vt_s[BACK_TILES + t] = rows_of(kv_ref.at[1], BACK_TILES + t, KS).T

    def q_block(i, _):
        qi = packet_rows(a_ref, i, IN_Q)
        gi = packet_rows(a_ref, i, IN_G)
        start, last, first, end, clear = block_of(i, st_ref, plan_ref)

        @pl.when(plan_ref[i] == 0)
        def _():
            lse, delta = forward_block(i, qi, gi, start, last, clear, first, end, kv_ref, vt_s, dq_s, a_s)
            lse_s[...] = lse
            delta_s[...] = delta
            dq_s[...] = jnp.zeros_like(dq_s)
            block_out(i, OUT_A, a_s, out_ref, sems.at[QB]).start()

        @pl.when(plan_ref[i] == 1)
        def _():
            lse_s[...] = lse_ref[i]
            delta_s[...] = delta_ref[i]
            dq_s[...] = dq_ref[i]

        grad_tiles(
            jnp.maximum(first, BACK_TILES),
            end,
            BACK_TILES,
            qi,
            gi,
            start,
            last,
            clear,
            lse_s[...],
            delta_s[...],
            kv_ref,
            kt_s,
            dk_s,
            dv_s,
            dq_s,
        )
        o_s[pl.ds(i * QS, QS)] = (dq_s[...] * SCALE).T.astype(BF).reshape(QS, HALF, HEAD)
        block_out(i, OUT_Q, o_s, out_ref, sems.at[i]).start()

        @pl.when(plan_ref[i] == 0)
        def _():
            block_out(i, OUT_A, a_s, out_ref, sems.at[QB]).wait()

        return 0

    lax.fori_loop(0, QB, q_block, 0)
    even = core == 0
    for t in range(OWN_TILES):
        dk, dv = dk_s[t] * SCALE, dv_s[t]
        half, s0 = t // (OWN_TILES // 2), (t % (OWN_TILES // 2)) * KS
        at = (slice(s0, s0 + KS), slice(half * HALF, half * HALF + HALF))
        keep_ref[at] = jnp.where(even, dk, dv).astype(BF).reshape(KS, HALF, HEAD)
        give_ref[at] = jnp.where(even, dv, dk).astype(BF).reshape(KS, HALF, HEAD)
    for i in range(QB):
        block_out(i, OUT_Q, o_s, out_ref, sems.at[i]).wait()


def tie_kernel(x_ref, after_ref, o_ref, sems):
    del x_ref, after_ref, o_ref, sems


def merge_kernel(keep_ref, got_ref, back_ref, old_ref, out_ref, x_s, sems):
    lower, upper = slice(0, HALF), slice(HALF, 2 * HALF)
    x_s[:, lower] = (keep_ref[:, lower].astype(F32) + got_ref[:, lower].astype(F32)).astype(BF)
    total = keep_ref[:, upper].astype(F32) + got_ref[:, upper].astype(F32)
    x_s[:, upper] = (total + back_ref[...].astype(F32)).astype(BF)
    finish(begin([(x_s, out_ref.at[:, pl.ds(OUT_X, 128)])], sems))


def unpack_kernel(t_ref, a_ref, q_ref, k_ref, v_ref, sems):
    pairs = []
    for n in range(HEADS):
        pairs.append((t_ref.at[n, pl.ds(OUT_A, 128)], a_ref.at[:, columns(n)]))
        pairs.append((t_ref.at[n, pl.ds(OUT_Q, 128)], q_ref.at[:, columns(n)]))
    copies = begin(pairs, sems)
    for g in range(GROUPS):
        at = slice(g * HEAD, (g + 1) * HEAD)
        for n, o_ref in ((4 * g, k_ref), (4 * g + 1, v_ref)):
            total = t_ref[n, OUT_X : OUT_X + 128].astype(F32) + t_ref[
                n + 2, OUT_X : OUT_X + 128
            ].astype(F32)
            o_ref[:, at] = total.astype(BF)
    finish(copies)


def shape(dims, dtype=BF):
    return jax.ShapeDtypeStruct(dims, dtype)


HBM = pl.BlockSpec(memory_space=pltpu.HBM)
VMEM = pl.BlockSpec(memory_space=pltpu.VMEM)
SMEM = pl.BlockSpec(memory_space=pltpu.SMEM)


def call(kernel, name, us, ins, outs, scratch, copies, mib=32, **more):
    return pl.pallas_call(
        kernel,
        in_specs=ins,
        out_specs=[space for space, _ in outs],
        out_shape=[what for _, what in outs],
        scratch_shapes=scratch + [pltpu.SemaphoreType.DMA((copies,))],
        compiler_params=pltpu.CompilerParams(vmem_limit_bytes=mib * 1024 * 1024),
        cost_estimate=pl.CostEstimate(
            flops=int(us * 4e8), bytes_accessed=1 << 20, transcendentals=0
        ),
        name=name,
        **more,
    )


def tie(x, after):
    (x,) = call(
        tie_kernel,
        "tie",
        1,
        [HBM, HBM],
        [(HBM, shape(x.shape))],
        [],
        1,
        input_output_aliases={0: 0},
    )(x, after)
    return x


def on_device(queries, key_states, value_vectors, grad_out, doc_start):
    cycle = lax.axis_index("dp")
    core = lax.axis_index("ctx") % 2
    q = queries.reshape(128, HEADS * HEAD)
    g = grad_out.reshape(128, HEADS * HEAD)
    k = key_states.reshape(128, GROUPS * HEAD)
    v = value_vectors.reshape(128, GROUPS * HEAD)
    swap = [(i, i ^ 1) for i in range(MEMBERS)]
    budget = jnp.where(cycle % 4 == 0, 0, jnp.where(cycle % 4 == 1, 64, 40))
    which = jnp.stack([core, budget])

    rel = doc_start.reshape(2, HALF) - (cycle * SPAN - BACK)
    parts = jnp.stack([rel // 64, rel % 64], axis=1).reshape(4, HALF).astype(BF)
    zero = jnp.zeros_like(parts)
    starts = jnp.where(
        core == 0,
        jnp.concatenate([parts, zero], axis=1),
        jnp.concatenate([zero, parts], axis=1),
    )
    starts = jnp.pad(starts, ((0, 12), (0, 0)))

    rows = pltpu.VMEM((2 * MEMBERS, HALF, HEAD), BF)
    wide = (VMEM, shape((QB, HEAD, TQ), F32))
    line = (VMEM, shape((QB, 1, TQ), F32))

    def turned(tiles):
        return pltpu.VMEM((tiles, HEAD, TK), BF)

    def sums(tiles):
        return pltpu.VMEM((tiles, TK, HEAD), F32)

    tail = jnp.concatenate([k[HALF:], v[HALF:]], axis=0)
    tail = lax.ppermute(tail, "dp", [(i, i + 1) for i in range(15)])
    packets = shape((HEADS, IN_ROWS, HEAD))
    (a,) = call(
        pack_kernel,
        "pack",
        1,
        [HBM, HBM, HBM, HBM],
        [(VMEM, packets)],
        [],
        3 * HEADS,
    )(*(pltpu.with_memory_space_constraint(each, pltpu.HBM) for each in (q, g, k, v)))
    (a,) = call(
        pack_tail_kernel,
        "pack_tail",
        1,
        [VMEM, VMEM, pl.BlockSpec(memory_space=pl.ANY)],
        [(pl.BlockSpec(memory_space=pl.ANY), packets)],
        [pltpu.VMEM((HEADS, HALF + 16, HEAD), BF)],
        1,
        input_output_aliases={2: 0},
    )(tail, starts, a)
    a = lax.all_to_all(a, "ctx", 0, 0, tiled=True)
    x = lax.ppermute(a[:, IN_X : IN_X + 192], "ctx", swap)
    st, kv, lse, delta, out, dq, keep_back, give_back, plan = call(
        forward_kernel,
        "forward",
        16,
        [SMEM, VMEM, VMEM],
        [
            (VMEM, shape((QB, 1, TQ), jnp.int32)),
            (VMEM, shape((2, 3 * MEMBERS, HALF, HEAD))),
            line,
            line,
            (HBM, shape((MEMBERS, OUT_ROWS, HEAD))),
            wide,
            (VMEM, shape((MEMBERS, HALF, HEAD))),
            (VMEM, shape((MEMBERS, HALF, HEAD))),
            (SMEM, shape((3 * QB,), jnp.int32)),
        ],
        [turned(BACK_TILES + OWN_TILES), turned(BACK_TILES), pltpu.VMEM((HEAD, TQ), F32), rows]
        + [sums(BACK_TILES), sums(BACK_TILES)],
        1,
    )(which, a, x)
    got_back = lax.ppermute(give_back, "ctx", swap)
    back = (keep_back.astype(F32) + got_back.astype(F32)).astype(BF)
    sent_back = lax.ppermute(back, "dp", [(i + 1, i) for i in range(15)])
    out, keep, give = call(
        own_kernel,
        "own",
        11,
        [SMEM, SMEM, VMEM, VMEM, VMEM, VMEM, VMEM, VMEM, HBM, HBM],
        [
            (HBM, shape((MEMBERS, OUT_ROWS, HEAD))),
            (VMEM, shape((MEMBERS, 128, HEAD))),
            (VMEM, shape((MEMBERS, 128, HEAD))),
        ],
        [
            turned(BACK_TILES + OWN_TILES),
            turned(OWN_TILES),
            pltpu.VMEM((1, TQ), F32),
            pltpu.VMEM((1, TQ), F32),
            pltpu.VMEM((HEAD, TQ), F32),
            rows,
            rows,
            sums(OWN_TILES),
            sums(OWN_TILES),
        ],
        QB + 1,
        input_output_aliases={8: 0},
    )(which, plan, a, kv, st, lse, delta, dq, out, back)
    got = lax.ppermute(tie(give, sent_back), "ctx", swap)
    (out,) = call(
        merge_kernel,
        "merge",
        1,
        [VMEM, VMEM, VMEM, HBM],
        [(HBM, shape((MEMBERS, OUT_ROWS, HEAD)))],
        [pltpu.VMEM((MEMBERS, 128, HEAD), BF)],
        1,
        input_output_aliases={3: 0},
    )(keep, got, sent_back, out)
    out = lax.all_to_all(out, "ctx", 0, 0, tiled=True)
    attn, q_grad, k_grad, v_grad = call(
        unpack_kernel,
        "unpack",
        2,
        [VMEM],
        [(HBM, shape(q.shape)), (HBM, shape(q.shape)), (VMEM, shape(k.shape)), (VMEM, shape(k.shape))],
        [],
        2 * HEADS,
    )(out)
    return (
        attn.reshape(queries.shape),
        q_grad.reshape(queries.shape),
        k_grad.reshape(key_states.shape),
        v_grad.reshape(value_vectors.shape),
    )


def solution(mesh):
    wide = P("dp", None, "ctx", None, None)
    return jax.shard_map(
        on_device,
        mesh=mesh,
        in_specs=(wide, wide, wide, wide, P("dp", None, "ctx", None)),
        out_specs=(wide, wide, wide, wide),
        check_vma=False,
    )
```

```python
from functools import partial

import jax
import jax.numpy as jnp
from jax import lax
from jax.experimental import pallas as pl
from jax.experimental.pallas import tpu as pltpu
from jax.sharding import PartitionSpec as P

HEAD = 128
HALF = 64
MEMBERS = 16
HEADS = 16
GROUPS = 4
SPAN = 2048
BACK = 1024
TQ = 512
TK = 512
QB = SPAN // TQ
QS = TQ // HALF
KS = TK // HALF
OWN_TILES = SPAN // TK
BACK_TILES = BACK // TK
SCALE = HEAD**-0.5
FOLD = SCALE * 1.4426950408889634
NEG = -1e30
BF = jnp.bfloat16
F32 = jnp.float32

IN_Q, IN_G, IN_X, IN_S, IN_ROWS = 0, 128, 256, 448, 464
OUT_A, OUT_Q, OUT_X, OUT_ROWS = 0, 128, 256, 384

NT = (((1,), (1,)), ((), ()))
NN = (((1,), (0,)), ((), ()))


def dot(a, b, dims=NN):
    return lax.dot_general(a, b, dims, preferred_element_type=F32)


def begin(pairs, sems):
    copies = [pltpu.make_async_copy(a, b, sems.at[i]) for i, (a, b) in enumerate(pairs)]
    for c in copies:
        c.start()
    return copies


def finish(copies):
    for c in copies:
        c.wait()


def columns(n):
    return pl.ds(n * HEAD, HEAD)


def pack_kernel(q_ref, g_ref, k_ref, v_ref, o_ref, sems):
    pairs = []
    for n in range(HEADS):
        x_ref = k_ref if n % 2 == 0 else v_ref
        pairs.append((q_ref.at[:, columns(n)], o_ref.at[n, pl.ds(IN_Q, 128)]))
        pairs.append((g_ref.at[:, columns(n)], o_ref.at[n, pl.ds(IN_G, 128)]))
        pairs.append((x_ref.at[:, columns(n // 4)], o_ref.at[n, pl.ds(IN_X, 128)]))
    finish(begin(pairs, sems))


def pack_tail_kernel(tail_ref, s_ref, old_ref, o_ref, x_s, sems):
    del old_ref
    for n in range(HEADS):
        row = (n % 2) * HALF
        x_s[n, 0:HALF] = tail_ref[row : row + HALF, n // 4 * HEAD : (n // 4 + 1) * HEAD]
        x_s[n, HALF : HALF + 16] = s_ref[...]
    finish(begin([(x_s, o_ref.at[:, pl.ds(IN_X + 128, HALF + 16)])], sems))


def low_position(i):
    source = (i - QB // 2) * QS + QS - 1
    upper = (2 * MEMBERS - 1 - source) * HALF
    return BACK + jnp.where(i >= QB // 2, upper, i * TQ)


def block_of(i, st_ref, plan_ref):
    lane = lax.broadcasted_iota(jnp.int32, (1, TQ), 1)
    part = lane // HALF
    part = jnp.where(i >= QB // 2, QS - 1 - part, part)
    low = low_position(i)
    end = (low + TQ - 1) // TK + 1
    whole = (plan_ref[2 * QB + i], low)
    return st_ref[i], low + part * HALF + lane % HALF, plan_ref[QB + i], end, whole


def masked(s, start, last, base, turned, fill=NEG):
    rows = lax.broadcasted_iota(jnp.int32, (HALF, TQ), 0)
    parts = []
    for b in range(KS):
        off = base + HALF * jnp.where(turned, KS - 1 - b, b)
        seen = (rows >= start - off) & (rows <= last - off)
        parts.append(jnp.where(seen, s[b * HALF : (b + 1) * HALF], fill))
    return jnp.concatenate(parts, axis=0)


def place(t):
    upper = t >= BACK_TILES + OWN_TILES // 2
    turned = (t < BACK_TILES) | upper
    top = jnp.where(upper, 2 * BACK_TILES + OWN_TILES + OWN_TILES // 2 - 1, BACK_TILES - 1)
    return jnp.where(turned, top - t, t), turned


def packet_rows(ref, i, row):
    half = pl.ds(pl.multiple_of(row + (i // 2) * HALF, HALF), HALF)
    return ref[pl.ds((i % 2) * QS, QS), half].reshape(TQ, HEAD)


def rows_of(ref, at, count):
    return ref[pl.ds(at * count, count)].reshape(count * HALF, HEAD)


def inside(whole, t):
    return (t * TK >= whole[0]) & (t * TK + TK - 1 <= whole[1])


def softmax_tiles(lo, hi, qi, start, last, clear, kv_s, vt_s, acc_s, p_s, m_s):
    acc_s[...] = jnp.zeros_like(acc_s)

    def tile(whole, t, m, l8):
        at, turned = place(t)
        s = dot(rows_of(kv_s.at[0], at, KS), qi, NT) * FOLD
        if not whole:
            s = masked(s, start, last, t * TK, turned)
        m_new = jnp.maximum(m, jnp.max(s, axis=0, keepdims=True))
        p = jnp.exp2(s - m_new)
        p_s[t] = p
        m_s[t] = m_new
        keep = jnp.exp2(m - m_new)
        l8 = l8 * keep + jnp.sum(p.reshape(TK // 8, 8, TQ), axis=0)
        acc_s[...] = acc_s[...] * keep + dot(vt_s[at], p.astype(BF))
        return m_new, l8

    def either(t, carry):
        return lax.cond(
            inside(clear, t), partial(tile, True), partial(tile, False), t, *carry
        )

    return lax.fori_loop(
        lo, hi, either, (jnp.full((1, TQ), NEG, F32), jnp.zeros((8, TQ), F32))
    )


def grad_tile(p, at, base, qi, gi, delta, kv_s, kt_s, dk_s, dv_s, dq_s):
    dp = dot(rows_of(kv_s.at[1], at, KS), gi, NT)
    at = at - base
    ds = (p * (dp - delta)).astype(BF)
    dv_s[at] += dot(p.astype(BF), gi)
    dk_s[at] += dot(ds, qi)
    dq_s[...] += dot(kt_s[at], ds)


def grad_tiles(lo, hi, base, qi, gi, start, last, clear, lse, delta, kv_s, kt_s, dk_s, dv_s, dq_s):
    def tile(whole, t):
        at, turned = place(t)
        s = dot(rows_of(kv_s.at[0], at, KS), qi, NT) * FOLD - lse
        if not whole:
            s = masked(s, start, last, t * TK, turned)
        grad_tile(jnp.exp2(s), at, base, qi, gi, delta, kv_s, kt_s, dk_s, dv_s, dq_s)
        return 0

    def either(t, _):
        return lax.cond(inside(clear, t), partial(tile, True), partial(tile, False), t)

    lax.fori_loop(lo, hi, either, 0)


def kept_tiles(lo, hi, base, qi, gi, lse, delta, kv_s, kt_s, dk_s, dv_s, dq_s, p_s, m_s):
    def tile(t, _):
        p = p_s[t] * jnp.exp2(m_s[t] - lse)
        grad_tile(p, place(t)[0], base, qi, gi, delta, kv_s, kt_s, dk_s, dv_s, dq_s)
        return 0

    lax.fori_loop(lo, hi, tile, 0)


def forward_block(i, qi, gi, start, last, clear, first, end, kv_s, vt_s, acc_s, p_s, m_s, out_ref):
    m, l8 = softmax_tiles(first, end, qi, start, last, clear, kv_s, vt_s, acc_s, p_s, m_s)
    l = jnp.sum(l8, axis=0, keepdims=True)
    out_t = acc_s[...] * (1.0 / l)
    delta = jnp.sum(out_t * gi.astype(F32).T, axis=0, keepdims=True)
    store_block(i, OUT_A, out_t.T.astype(BF), out_ref)
    return m + jnp.log2(l), delta


def store_block(i, row, value, out_ref):
    half = pl.ds(pl.multiple_of(row + (i // 2) * HALF, HALF), HALF)
    out_ref[pl.ds((i % 2) * QS, QS), half] = value.reshape(QS, HALF, HEAD)


def block_out(i, row, o_s, out_ref, sem):
    at = (
        pl.ds((i % 2) * QS, QS),
        pl.ds(pl.multiple_of(row + (i // 2) * HALF, HALF), HALF),
    )
    return pltpu.make_async_copy(o_s.at[at], out_ref.at[at], sem)


def forward_kernel(
    core_ref, a_ref, x_ref,
    st_ref, kv_s, lse_ref, delta_ref, out_ref, dq_ref, keep_ref, give_ref, plan_ref,
    vt_s, kt_s, acc_s, p_s, m_s, dk_s, dv_s, sems,
):
    del sems
    core = core_ref[0]
    for part, row in enumerate((128, 0, HALF)):
        at = slice(part * MEMBERS, (part + 1) * MEMBERS)
        mine = a_ref[:, IN_X + row : IN_X + row + HALF]
        theirs = x_ref[:, row : row + HALF]
        kv_s[0, at] = jnp.where(core == 0, mine, theirs)
        kv_s[1, at] = jnp.where(core == 0, theirs, mine)
    for t in range(SPAN // 128):
        s0, row = (2 * t, 0) if t < 8 else (2 * t - 16, 2)
        both = a_ref[s0, IN_S : IN_S + 16].astype(F32) + a_ref[s0 + 1, IN_S : IN_S + 16].astype(F32)
        start = both[row : row + 1] * 64.0 + both[row + 1 : row + 2]
        c = (t % 4) * 128
        st_ref[t // 4, 0:1, c : c + 128] = start.astype(jnp.int32)
    for t in range(BACK_TILES + OWN_TILES):
        vt_s[t] = rows_of(kv_s.at[1], t, KS).T
    for t in range(BACK_TILES):
        kt_s[t] = rows_of(kv_s.at[0], t, KS).T
    dk_s[...] = jnp.zeros_like(dk_s)
    dv_s[...] = jnp.zeros_like(dv_s)

    spans = []
    for i in range(QB):
        first = jnp.min(st_ref[i]) // TK
        plan_ref[QB + i] = first
        plan_ref[2 * QB + i] = jnp.max(st_ref[i])
        spans.append((first, (low_position(i) + TQ - 1) // TK + 1))
    budget = core_ref[1]
    for first, end in spans:
        reach = jnp.maximum(BACK_TILES - first, 0)
        budget -= jnp.where(reach > 0, 4 * (end - first) + 5 * reach + 2, 0)
    for i, (first, end) in enumerate(spans):
        need = 4 * (end - first) + 2
        extra = (first >= BACK_TILES) & (need <= budget)
        budget -= jnp.where(extra, need, 0)
        plan_ref[i] = ((first < BACK_TILES) | extra).astype(jnp.int32)

    def q_block(i, _):
        @pl.when(plan_ref[i] == 1)
        def _():
            start, last, first, end, clear = block_of(i, st_ref, plan_ref)
            qi = packet_rows(a_ref, i, IN_Q)
            gi = packet_rows(a_ref, i, IN_G)
            lse, delta = forward_block(
                i, qi, gi, start, last, clear, first, end, kv_s, vt_s, acc_s, p_s, m_s, out_ref
            )
            lse_ref[i] = lse
            delta_ref[i] = delta
            dq_ref[i] = jnp.zeros((HEAD, TQ), F32)
            kept_tiles(
                first,
                BACK_TILES,
                0,
                qi,
                gi,
                lse,
                delta,
                kv_s,
                kt_s,
                dk_s,
                dv_s,
                dq_ref.at[i],
                p_s,
                m_s,
            )

        return 0

    lax.fori_loop(0, QB, q_block, 0)
    even = core == 0
    for t in range(BACK_TILES):
        dk, dv = dk_s[t] * SCALE, dv_s[t]
        at = slice(t * KS, (t + 1) * KS)
        keep_ref[at] = jnp.where(even, dk, dv).astype(BF).reshape(KS, HALF, HEAD)
        give_ref[at] = jnp.where(even, dv, dk).astype(BF).reshape(KS, HALF, HEAD)


def own_kernel(
    core_ref, plan_ref, a_ref, kv_ref, st_ref, lse_ref, delta_ref, dq_ref, old_ref, after_ref,
    out_ref, keep_ref, give_ref,
    vt_s, kt_s, acc_s, p_s, m_s, dq_s, o_s, dk_s, dv_s, sems,
):
    del old_ref, after_ref
    core = core_ref[0]
    dk_s[...] = jnp.zeros_like(dk_s)
    dv_s[...] = jnp.zeros_like(dv_s)
    for t in range(OWN_TILES):
        kt_s[t] = rows_of(kv_ref.at[0], BACK_TILES + t, KS).T
        vt_s[BACK_TILES + t] = rows_of(kv_ref.at[1], BACK_TILES + t, KS).T

    def q_block(i, _):
        qi = packet_rows(a_ref, i, IN_Q)
        gi = packet_rows(a_ref, i, IN_G)
        start, last, first, end, clear = block_of(i, st_ref, plan_ref)

        low = jnp.maximum(first, BACK_TILES)

        @pl.when(plan_ref[i] == 0)
        def _():
            lse, delta = forward_block(
                i, qi, gi, start, last, clear, first, end, kv_ref, vt_s, acc_s, p_s, m_s, o_s
            )
            dq_s[...] = jnp.zeros_like(dq_s)
            kept_tiles(
                low,
                end,
                BACK_TILES,
                qi,
                gi,
                lse,
                delta,
                kv_ref,
                kt_s,
                dk_s,
                dv_s,
                dq_s,
                p_s,
                m_s,
            )

        @pl.when(plan_ref[i] == 1)
        def _():
            dq_s[...] = dq_ref[i]
            grad_tiles(
                low,
                end,
                BACK_TILES,
                qi,
                gi,
                start,
                last,
                clear,
                lse_ref[i],
                delta_ref[i],
                kv_ref,
                kt_s,
                dk_s,
                dv_s,
                dq_s,
            )

        store_block(i, OUT_Q, (dq_s[...] * SCALE).T.astype(BF), o_s)
        block_out(i, OUT_Q, o_s, out_ref, sems.at[i]).start()

        @pl.when(plan_ref[i] == 0)
        def _():
            copy = block_out(i, OUT_A, o_s, out_ref, sems.at[QB])
            copy.start()
            copy.wait()

        return 0

    lax.fori_loop(0, QB, q_block, 0)
    for i in range(QB):
        block_out(i, OUT_Q, o_s, out_ref, sems.at[i]).wait()
    even = core == 0
    for t in range(OWN_TILES):
        dk, dv = dk_s[t] * SCALE, dv_s[t]
        half, s0 = t // (OWN_TILES // 2), (t % (OWN_TILES // 2)) * KS
        at = (slice(s0, s0 + KS), slice(half * HALF, half * HALF + HALF))
        keep_ref[at] = jnp.where(even, dk, dv).astype(BF).reshape(KS, HALF, HEAD)
        give_ref[at] = jnp.where(even, dv, dk).astype(BF).reshape(KS, HALF, HEAD)


def tie_kernel(x_ref, after_ref, o_ref, sems):
    del x_ref, after_ref, o_ref, sems


def merge_kernel(keep_ref, got_ref, back_ref, old_ref, out_ref, x_s, sems):
    lower, upper = slice(0, HALF), slice(HALF, 2 * HALF)
    x_s[:, lower] = (keep_ref[:, lower].astype(F32) + got_ref[:, lower].astype(F32)).astype(BF)
    total = keep_ref[:, upper].astype(F32) + got_ref[:, upper].astype(F32)
    x_s[:, upper] = (total + back_ref[...].astype(F32)).astype(BF)
    finish(begin([(x_s, out_ref.at[:, pl.ds(OUT_X, 128)])], sems))


def unpack_kernel(t_ref, a_ref, q_ref, k_ref, v_ref, sems):
    pairs = []
    for n in range(HEADS):
        pairs.append((t_ref.at[n, pl.ds(OUT_A, 128)], a_ref.at[:, columns(n)]))
        pairs.append((t_ref.at[n, pl.ds(OUT_Q, 128)], q_ref.at[:, columns(n)]))
    copies = begin(pairs, sems)
    for g in range(GROUPS):
        at = slice(g * HEAD, (g + 1) * HEAD)
        for n, o_ref in ((4 * g, k_ref), (4 * g + 1, v_ref)):
            total = t_ref[n, OUT_X : OUT_X + 128].astype(F32) + t_ref[
                n + 2, OUT_X : OUT_X + 128
            ].astype(F32)
            o_ref[:, at] = total.astype(BF)
    finish(copies)


def shape(dims, dtype=BF):
    return jax.ShapeDtypeStruct(dims, dtype)


HBM = pl.BlockSpec(memory_space=pltpu.HBM)
VMEM = pl.BlockSpec(memory_space=pltpu.VMEM)
SMEM = pl.BlockSpec(memory_space=pltpu.SMEM)


def call(kernel, name, us, ins, outs, scratch, copies, mib=32, **more):
    return pl.pallas_call(
        kernel,
        in_specs=ins,
        out_specs=[space for space, _ in outs],
        out_shape=[what for _, what in outs],
        scratch_shapes=scratch + [pltpu.SemaphoreType.DMA((copies,))],
        compiler_params=pltpu.CompilerParams(vmem_limit_bytes=mib * 1024 * 1024),
        cost_estimate=pl.CostEstimate(
            flops=int(us * 4e8), bytes_accessed=1 << 20, transcendentals=0
        ),
        name=name,
        **more,
    )


def tie(x, after):
    (x,) = call(
        tie_kernel,
        "tie",
        1,
        [HBM, HBM],
        [(HBM, shape(x.shape))],
        [],
        1,
        input_output_aliases={0: 0},
    )(x, after)
    return x


def on_device(queries, key_states, value_vectors, grad_out, doc_start):
    cycle = lax.axis_index("dp")
    core = lax.axis_index("ctx") % 2
    q = queries.reshape(128, HEADS * HEAD)
    g = grad_out.reshape(128, HEADS * HEAD)
    k = key_states.reshape(128, GROUPS * HEAD)
    v = value_vectors.reshape(128, GROUPS * HEAD)
    swap = [(i, i ^ 1) for i in range(MEMBERS)]
    budget = jnp.where(cycle % 4 == 0, 0, jnp.where(cycle % 4 == 1, 64, 40))
    which = jnp.stack([core, budget])

    rel = doc_start.reshape(2, HALF) - (cycle * SPAN - BACK)
    parts = jnp.stack([rel // 64, rel % 64], axis=1).reshape(4, HALF).astype(BF)
    zero = jnp.zeros_like(parts)
    starts = jnp.where(
        core == 0,
        jnp.concatenate([parts, zero], axis=1),
        jnp.concatenate([zero, parts], axis=1),
    )
    starts = jnp.pad(starts, ((0, 12), (0, 0)))

    wide = (VMEM, shape((QB, HEAD, TQ), F32))
    line = (VMEM, shape((QB, 1, TQ), F32))

    def turned(tiles):
        return pltpu.VMEM((tiles, HEAD, TK), BF)

    def sums(tiles):
        return pltpu.VMEM((tiles, TK, HEAD), F32)

    tail = jnp.concatenate([k[HALF:], v[HALF:]], axis=0)
    tail = lax.ppermute(tail, "dp", [(i, i + 1) for i in range(15)])
    kept = [
        pltpu.VMEM((BACK_TILES + OWN_TILES, TK, TQ), F32),
        pltpu.VMEM((BACK_TILES + OWN_TILES, 1, TQ), F32),
    ]
    packets = shape((HEADS, IN_ROWS, HEAD))
    (a,) = call(
        pack_kernel,
        "pack",
        1,
        [HBM, HBM, HBM, HBM],
        [(VMEM, packets)],
        [],
        3 * HEADS,
    )(*(pltpu.with_memory_space_constraint(each, pltpu.HBM) for each in (q, g, k, v)))
    (a,) = call(
        pack_tail_kernel,
        "pack_tail",
        1,
        [VMEM, VMEM, pl.BlockSpec(memory_space=pl.ANY)],
        [(pl.BlockSpec(memory_space=pl.ANY), packets)],
        [pltpu.VMEM((HEADS, HALF + 16, HEAD), BF)],
        1,
        input_output_aliases={2: 0},
    )(tail, starts, a)
    a = lax.all_to_all(a, "ctx", 0, 0, tiled=True)
    x = lax.ppermute(a[:, IN_X : IN_X + 192], "ctx", swap)
    st, kv, lse, delta, out, dq, keep_back, give_back, plan = call(
        forward_kernel,
        "forward",
        16,
        [SMEM, VMEM, VMEM],
        [
            (VMEM, shape((QB, 1, TQ), jnp.int32)),
            (VMEM, shape((2, 3 * MEMBERS, HALF, HEAD))),
            line,
            line,
            (VMEM, shape((MEMBERS, OUT_ROWS, HEAD))),
            wide,
            (VMEM, shape((MEMBERS, HALF, HEAD))),
            (VMEM, shape((MEMBERS, HALF, HEAD))),
            (SMEM, shape((3 * QB,), jnp.int32)),
        ],
        [turned(BACK_TILES + OWN_TILES), turned(BACK_TILES), pltpu.VMEM((HEAD, TQ), F32)]
        + kept
        + [sums(BACK_TILES), sums(BACK_TILES)],
        1,
    )(which, a, x)
    got_back = lax.ppermute(give_back, "ctx", swap)
    back = (keep_back.astype(F32) + got_back.astype(F32)).astype(BF)
    sent_back = lax.ppermute(back, "dp", [(i + 1, i) for i in range(15)])
    out, keep, give = call(
        own_kernel,
        "own",
        11,
        [SMEM, SMEM, VMEM, VMEM, VMEM, VMEM, VMEM, VMEM, HBM, HBM],
        [
            (HBM, shape((MEMBERS, OUT_ROWS, HEAD))),
            (VMEM, shape((MEMBERS, 128, HEAD))),
            (VMEM, shape((MEMBERS, 128, HEAD))),
        ],
        [
            turned(BACK_TILES + OWN_TILES),
            turned(OWN_TILES),
            pltpu.VMEM((HEAD, TQ), F32),
            *kept,
            pltpu.VMEM((HEAD, TQ), F32),
            pltpu.VMEM((MEMBERS, OUT_X, HEAD), BF),
            sums(OWN_TILES),
            sums(OWN_TILES),
        ],
        QB + 1,
        input_output_aliases={8: 0},
    )(which, plan, a, kv, st, lse, delta, dq, out, back)
    got = lax.ppermute(tie(give, sent_back), "ctx", swap)
    (out,) = call(
        merge_kernel,
        "merge",
        1,
        [VMEM, VMEM, VMEM, HBM],
        [(HBM, shape((MEMBERS, OUT_ROWS, HEAD)))],
        [pltpu.VMEM((MEMBERS, 128, HEAD), BF)],
        1,
        input_output_aliases={3: 0},
    )(keep, got, sent_back, out)
    out = lax.all_to_all(out, "ctx", 0, 0, tiled=True)
    attn, q_grad, k_grad, v_grad = call(
        unpack_kernel,
        "unpack",
        2,
        [VMEM],
        [(HBM, shape(q.shape)), (HBM, shape(q.shape)), (VMEM, shape(k.shape)), (VMEM, shape(k.shape))],
        [],
        2 * HEADS,
    )(out)
    return (
        attn.reshape(queries.shape),
        q_grad.reshape(queries.shape),
        k_grad.reshape(key_states.shape),
        v_grad.reshape(value_vectors.shape),
    )


def solution(mesh):
    wide = P("dp", None, "ctx", None, None)
    return jax.shard_map(
        on_device,
        mesh=mesh,
        in_specs=(wide, wide, wide, wide, P("dp", None, "ctx", None)),
        out_specs=(wide, wide, wide, wide),
        check_vma=False,
    )
```

```python
from functools import partial

import jax
import jax.numpy as jnp
from jax import lax
from jax.experimental import pallas as pl
from jax.experimental.pallas import tpu as pltpu
from jax.sharding import PartitionSpec as P

HEAD = 128
HALF = 64
MEMBERS = 16
HEADS = 16
GROUPS = 4
SPAN = 2048
BACK = 1024
TQ = 512
TK = 512
QB = SPAN // TQ
QS = TQ // HALF
KS = TK // HALF
OWN_TILES = SPAN // TK
BACK_TILES = BACK // TK
SCALE = HEAD**-0.5
FOLD = SCALE * 1.4426950408889634
NEG = -1e30
PIECES = 4
BF = jnp.bfloat16
F32 = jnp.float32

IN_Q, IN_G, IN_X, IN_S, IN_ROWS = 0, 128, 256, 448, 464
OUT_A, OUT_Q, OUT_X, OUT_ROWS = 0, 128, 256, 384

NT = (((1,), (1,)), ((), ()))
NN = (((1,), (0,)), ((), ()))


def dot(a, b, dims=NN):
    return lax.dot_general(a, b, dims, preferred_element_type=F32)


def begin(pairs, sems):
    copies = [pltpu.make_async_copy(a, b, sems.at[i]) for i, (a, b) in enumerate(pairs)]
    for c in copies:
        c.start()
    return copies


def finish(copies):
    for c in copies:
        c.wait()


def columns(n):
    return pl.ds(n * HEAD, HEAD)


def pack_kernel(q_ref, g_ref, k_ref, v_ref, o_ref, sems):
    pairs = []
    for n in range(HEADS):
        x_ref = k_ref if n % 2 == 0 else v_ref
        pairs.append((q_ref.at[:, columns(n)], o_ref.at[n, pl.ds(IN_Q, 128)]))
        pairs.append((g_ref.at[:, columns(n)], o_ref.at[n, pl.ds(IN_G, 128)]))
        pairs.append((x_ref.at[:, columns(n // 4)], o_ref.at[n, pl.ds(IN_X, 128)]))
    finish(begin(pairs, sems))


def pack_tail_kernel(tail_ref, s_ref, old_ref, o_ref, x_s, sems):
    del old_ref
    for n in range(HEADS):
        row = (n % 2) * HALF
        x_s[n, 0:HALF] = tail_ref[row : row + HALF, n // 4 * HEAD : (n // 4 + 1) * HEAD]
        x_s[n, HALF : HALF + 16] = s_ref[...]
    finish(begin([(x_s, o_ref.at[:, pl.ds(IN_X + 128, HALF + 16)])], sems))


def low_position(i):
    source = (i - QB // 2) * QS + QS - 1
    upper = (2 * MEMBERS - 1 - source) * HALF
    return BACK + jnp.where(i >= QB // 2, upper, i * TQ)


def block_of(i, st_ref, plan_ref):
    lane = lax.broadcasted_iota(jnp.int32, (1, TQ), 1)
    part = lane // HALF
    part = jnp.where(i >= QB // 2, QS - 1 - part, part)
    low = low_position(i)
    end = (low + TQ - 1) // TK + 1
    whole = (plan_ref[2 * QB + i], low)
    return st_ref[i], low + part * HALF + lane % HALF, plan_ref[QB + i], end, whole


def masked(s, start, last, base, turned, fill=NEG):
    rows = lax.broadcasted_iota(jnp.int32, (HALF, TQ), 0)
    parts = []
    for b in range(KS):
        off = base + HALF * jnp.where(turned, KS - 1 - b, b)
        seen = (rows >= start - off) & (rows <= last - off)
        parts.append(jnp.where(seen, s[b * HALF : (b + 1) * HALF], fill))
    return jnp.concatenate(parts, axis=0)


def place(t):
    upper = t >= BACK_TILES + OWN_TILES // 2
    turned = (t < BACK_TILES) | upper
    top = jnp.where(upper, 2 * BACK_TILES + OWN_TILES + OWN_TILES // 2 - 1, BACK_TILES - 1)
    return jnp.where(turned, top - t, t), turned


def packet_rows(ref, i, row):
    half = pl.ds(pl.multiple_of(row + (i // 2) * HALF, HALF), HALF)
    return ref[pl.ds((i % 2) * QS, QS), half].reshape(TQ, HEAD)


def rows_of(ref, at, count):
    return ref[pl.ds(at * count, count)].reshape(count * HALF, HEAD)


def inside(whole, t):
    return (t * TK >= whole[0]) & (t * TK + TK - 1 <= whole[1])


def softmax_tiles(lo, hi, qi, start, last, clear, kv_s, vt_s, acc_s, p_s, m_s):
    acc_s[...] = jnp.zeros_like(acc_s)

    def tile(whole, t, m, l8):
        at, turned = place(t)
        s = dot(rows_of(kv_s.at[0], at, KS), qi, NT) * FOLD
        if not whole:
            s = masked(s, start, last, t * TK, turned)
        m_new = jnp.maximum(m, jnp.max(s, axis=0, keepdims=True))
        p = jnp.exp2(s - m_new)
        p_s[t] = p
        m_s[t] = m_new
        keep = jnp.exp2(m - m_new)
        l8 = l8 * keep + jnp.sum(p.reshape(TK // 8, 8, TQ), axis=0)
        acc_s[...] = acc_s[...] * keep + dot(vt_s[at], p.astype(BF))
        return m_new, l8

    def either(t, carry):
        return lax.cond(
            inside(clear, t), partial(tile, True), partial(tile, False), t, *carry
        )

    return lax.fori_loop(
        lo, hi, either, (jnp.full((1, TQ), NEG, F32), jnp.zeros((8, TQ), F32))
    )


def grad_tile(p, at, base, qi, gi, delta, kv_s, kt_s, dk_s, dv_s, dq_s):
    dp = dot(rows_of(kv_s.at[1], at, KS), gi, NT)
    at = at - base
    ds = (p * (dp - delta)).astype(BF)
    dv_s[at] += dot(p.astype(BF), gi)
    dk_s[at] += dot(ds, qi)
    dq_s[...] += dot(kt_s[at], ds)


def grad_tiles(lo, hi, base, qi, gi, start, last, clear, lse, delta, kv_s, kt_s, dk_s, dv_s, dq_s):
    def tile(whole, t):
        at, turned = place(t)
        s = dot(rows_of(kv_s.at[0], at, KS), qi, NT) * FOLD - lse
        if not whole:
            s = masked(s, start, last, t * TK, turned)
        grad_tile(jnp.exp2(s), at, base, qi, gi, delta, kv_s, kt_s, dk_s, dv_s, dq_s)
        return 0

    def either(t, _):
        return lax.cond(inside(clear, t), partial(tile, True), partial(tile, False), t)

    lax.fori_loop(lo, hi, either, 0)


def kept_tiles(lo, hi, base, qi, gi, lse, delta, kv_s, kt_s, dk_s, dv_s, dq_s, p_s, m_s):
    def tile(t, _):
        p = p_s[t] * jnp.exp2(m_s[t] - lse)
        grad_tile(p, place(t)[0], base, qi, gi, delta, kv_s, kt_s, dk_s, dv_s, dq_s)
        return 0

    lax.fori_loop(lo, hi, tile, 0)


def forward_block(i, qi, gi, start, last, clear, first, end, kv_s, vt_s, acc_s, p_s, m_s, out_ref):
    m, l8 = softmax_tiles(first, end, qi, start, last, clear, kv_s, vt_s, acc_s, p_s, m_s)
    l = jnp.sum(l8, axis=0, keepdims=True)
    out_t = acc_s[...] * (1.0 / l)
    delta = jnp.sum(out_t * gi.astype(F32).T, axis=0, keepdims=True)
    store_block(i, OUT_A, out_t.T.astype(BF), out_ref)
    return m + jnp.log2(l), delta


def store_block(i, row, value, out_ref):
    half = pl.ds(pl.multiple_of(row + (i // 2) * HALF, HALF), HALF)
    out_ref[pl.ds((i % 2) * QS, QS), half] = value.reshape(QS, HALF, HEAD)


def block_out(i, row, o_s, out_ref, sem):
    at = (
        pl.ds((i % 2) * QS, QS),
        pl.ds(pl.multiple_of(row + (i // 2) * HALF, HALF), HALF),
    )
    return pltpu.make_async_copy(o_s.at[at], out_ref.at[at], sem)


def forward_kernel(
    core_ref, a_ref, x_ref,
    st_ref, kv_s, lse_ref, delta_ref, out_ref, dq_ref, keep_ref, give_ref, plan_ref,
    vt_s, kt_s, acc_s, p_s, m_s, dk_s, dv_s, sems,
):
    del sems
    core = core_ref[0]
    for part, row in enumerate((128, 0, HALF)):
        at = slice(part * MEMBERS, (part + 1) * MEMBERS)
        mine = a_ref[:, IN_X + row : IN_X + row + HALF]
        theirs = x_ref[:, row : row + HALF]
        kv_s[0, at] = jnp.where(core == 0, mine, theirs)
        kv_s[1, at] = jnp.where(core == 0, theirs, mine)
    for t in range(SPAN // 128):
        s0, row = (2 * t, 0) if t < 8 else (2 * t - 16, 2)
        both = a_ref[s0, IN_S : IN_S + 16].astype(F32) + a_ref[s0 + 1, IN_S : IN_S + 16].astype(F32)
        start = both[row : row + 1] * 64.0 + both[row + 1 : row + 2]
        c = (t % 4) * 128
        st_ref[t // 4, 0:1, c : c + 128] = start.astype(jnp.int32)
    for t in range(BACK_TILES + OWN_TILES):
        vt_s[t] = rows_of(kv_s.at[1], t, KS).T
    for t in range(BACK_TILES):
        kt_s[t] = rows_of(kv_s.at[0], t, KS).T
    dk_s[...] = jnp.zeros_like(dk_s)
    dv_s[...] = jnp.zeros_like(dv_s)

    spans = []
    for i in range(QB):
        first = jnp.min(st_ref[i]) // TK
        plan_ref[QB + i] = first
        plan_ref[2 * QB + i] = jnp.max(st_ref[i])
        spans.append((first, (low_position(i) + TQ - 1) // TK + 1))
    budget = core_ref[1]
    for first, end in spans:
        reach = jnp.maximum(BACK_TILES - first, 0)
        budget -= jnp.where(reach > 0, 4 * (end - first) + 5 * reach + 2, 0)
    for i, (first, end) in enumerate(spans):
        need = 4 * (end - first) + 2
        extra = (first >= BACK_TILES) & (need <= budget)
        budget -= jnp.where(extra, need, 0)
        plan_ref[i] = ((first < BACK_TILES) | extra).astype(jnp.int32)

    def q_block(i, _):
        @pl.when(plan_ref[i] == 1)
        def _():
            start, last, first, end, clear = block_of(i, st_ref, plan_ref)
            qi = packet_rows(a_ref, i, IN_Q)
            gi = packet_rows(a_ref, i, IN_G)
            lse, delta = forward_block(
                i, qi, gi, start, last, clear, first, end, kv_s, vt_s, acc_s, p_s, m_s, out_ref
            )
            lse_ref[i] = lse
            delta_ref[i] = delta
            dq_ref[i] = jnp.zeros((HEAD, TQ), F32)
            kept_tiles(
                first,
                BACK_TILES,
                0,
                qi,
                gi,
                lse,
                delta,
                kv_s,
                kt_s,
                dk_s,
                dv_s,
                dq_ref.at[i],
                p_s,
                m_s,
            )

        return 0

    lax.fori_loop(0, QB, q_block, 0)
    even = core == 0
    for t in range(BACK_TILES):
        dk, dv = dk_s[t] * SCALE, dv_s[t]
        at = slice(t * KS, (t + 1) * KS)
        keep_ref[at] = jnp.where(even, dk, dv).astype(BF).reshape(KS, HALF, HEAD)
        give_ref[at] = jnp.where(even, dv, dk).astype(BF).reshape(KS, HALF, HEAD)


def own_kernel(
    core_ref, plan_ref, a_ref, kv_ref, st_ref, lse_ref, delta_ref, dq_ref, old_ref, after_ref,
    out_ref, keep_ref, *rest,
):
    del old_ref, after_ref
    give_refs, rest = rest[:PIECES], rest[PIECES:]
    vt_s, kt_s, acc_s, p_s, m_s, dq_s, o_s, dk_s, dv_s, sems = rest
    core = core_ref[0]
    dk_s[...] = jnp.zeros_like(dk_s)
    dv_s[...] = jnp.zeros_like(dv_s)
    for t in range(OWN_TILES):
        kt_s[t] = rows_of(kv_ref.at[0], BACK_TILES + t, KS).T
        vt_s[BACK_TILES + t] = rows_of(kv_ref.at[1], BACK_TILES + t, KS).T

    def q_block(i, _):
        qi = packet_rows(a_ref, i, IN_Q)
        gi = packet_rows(a_ref, i, IN_G)
        start, last, first, end, clear = block_of(i, st_ref, plan_ref)

        low = jnp.maximum(first, BACK_TILES)

        @pl.when(plan_ref[i] == 0)
        def _():
            lse, delta = forward_block(
                i, qi, gi, start, last, clear, first, end, kv_ref, vt_s, acc_s, p_s, m_s, o_s
            )
            dq_s[...] = jnp.zeros_like(dq_s)
            kept_tiles(
                low,
                end,
                BACK_TILES,
                qi,
                gi,
                lse,
                delta,
                kv_ref,
                kt_s,
                dk_s,
                dv_s,
                dq_s,
                p_s,
                m_s,
            )

        @pl.when(plan_ref[i] == 1)
        def _():
            dq_s[...] = dq_ref[i]
            grad_tiles(
                low,
                end,
                BACK_TILES,
                qi,
                gi,
                start,
                last,
                clear,
                lse_ref[i],
                delta_ref[i],
                kv_ref,
                kt_s,
                dk_s,
                dv_s,
                dq_s,
            )

        store_block(i, OUT_Q, (dq_s[...] * SCALE).T.astype(BF), o_s)
        block_out(i, OUT_Q, o_s, out_ref, sems.at[i]).start()

        @pl.when(plan_ref[i] == 0)
        def _():
            copy = block_out(i, OUT_A, o_s, out_ref, sems.at[QB])
            copy.start()
            copy.wait()

        return 0

    lax.fori_loop(0, QB, q_block, 0)
    for i in range(QB):
        block_out(i, OUT_Q, o_s, out_ref, sems.at[i]).wait()
    even = core == 0
    for t in range(OWN_TILES):
        dk, dv = dk_s[t] * SCALE, dv_s[t]
        half, s0 = t // (OWN_TILES // 2), (t % (OWN_TILES // 2)) * KS
        at = (slice(s0, s0 + KS), slice(half * HALF, half * HALF + HALF))
        keep_ref[at] = jnp.where(even, dk, dv).astype(BF).reshape(KS, HALF, HEAD)
        given = jnp.where(even, dv, dk).astype(BF).reshape(KS, HALF, HEAD)
        for b in range(KS):
            piece, row = divmod(t * KS + b, 2 * MEMBERS // PIECES)
            give_refs[piece][row] = given[b]


def tie_kernel(x_ref, after_ref, o_ref, sems):
    del x_ref, after_ref, o_ref, sems


def merge_kernel(keep_ref, back_ref, old_ref, *rest):
    del old_ref
    got_refs, (out_ref, x_s, sems) = rest[:PIECES], rest[PIECES:]
    count = 2 * MEMBERS // PIECES
    for piece, got_ref in enumerate(got_refs):
        half, s0 = divmod(piece * count, MEMBERS)
        at = (slice(s0, s0 + count), slice(half * HALF, half * HALF + HALF))
        total = keep_ref[at].astype(F32) + got_ref[...].astype(F32)
        if half == 1:
            total = total + back_ref[s0 : s0 + count].astype(F32)
        x_s[at] = total.astype(BF)
    finish(begin([(x_s, out_ref.at[:, pl.ds(OUT_X, 128)])], sems))


def unpack_kernel(t_ref, a_ref, q_ref, k_ref, v_ref, sems):
    pairs = []
    for n in range(HEADS):
        pairs.append((t_ref.at[n, pl.ds(OUT_A, 128)], a_ref.at[:, columns(n)]))
        pairs.append((t_ref.at[n, pl.ds(OUT_Q, 128)], q_ref.at[:, columns(n)]))
    copies = begin(pairs, sems)
    for g in range(GROUPS):
        at = slice(g * HEAD, (g + 1) * HEAD)
        for n, o_ref in ((4 * g, k_ref), (4 * g + 1, v_ref)):
            total = t_ref[n, OUT_X : OUT_X + 128].astype(F32) + t_ref[
                n + 2, OUT_X : OUT_X + 128
            ].astype(F32)
            o_ref[:, at] = total.astype(BF)
    finish(copies)


def shape(dims, dtype=BF):
    return jax.ShapeDtypeStruct(dims, dtype)


HBM = pl.BlockSpec(memory_space=pltpu.HBM)
VMEM = pl.BlockSpec(memory_space=pltpu.VMEM)
SMEM = pl.BlockSpec(memory_space=pltpu.SMEM)


def call(kernel, name, us, ins, outs, scratch, copies, mib=32, **more):
    return pl.pallas_call(
        kernel,
        in_specs=ins,
        out_specs=[space for space, _ in outs],
        out_shape=[what for _, what in outs],
        scratch_shapes=scratch + [pltpu.SemaphoreType.DMA((copies,))],
        compiler_params=pltpu.CompilerParams(vmem_limit_bytes=mib * 1024 * 1024),
        cost_estimate=pl.CostEstimate(
            flops=int(us * 4e8), bytes_accessed=1 << 20, transcendentals=0
        ),
        name=name,
        **more,
    )


def tie(x, after):
    (x,) = call(
        tie_kernel,
        "tie",
        1,
        [HBM, HBM],
        [(HBM, shape(x.shape))],
        [],
        1,
        input_output_aliases={0: 0},
    )(x, after)
    return x


def on_device(queries, key_states, value_vectors, grad_out, doc_start):
    cycle = lax.axis_index("dp")
    core = lax.axis_index("ctx") % 2
    q = queries.reshape(128, HEADS * HEAD)
    g = grad_out.reshape(128, HEADS * HEAD)
    k = key_states.reshape(128, GROUPS * HEAD)
    v = value_vectors.reshape(128, GROUPS * HEAD)
    swap = [(i, i ^ 1) for i in range(MEMBERS)]
    budget = jnp.where(cycle % 4 == 0, 0, jnp.where(cycle % 4 == 1, 64, 40))
    which = jnp.stack([core, budget])

    rel = doc_start.reshape(2, HALF) - (cycle * SPAN - BACK)
    parts = jnp.stack([rel // 64, rel % 64], axis=1).reshape(4, HALF).astype(BF)
    zero = jnp.zeros_like(parts)
    starts = jnp.where(
        core == 0,
        jnp.concatenate([parts, zero], axis=1),
        jnp.concatenate([zero, parts], axis=1),
    )
    starts = jnp.pad(starts, ((0, 12), (0, 0)))

    wide = (VMEM, shape((QB, HEAD, TQ), F32))
    line = (VMEM, shape((QB, 1, TQ), F32))

    def turned(tiles):
        return pltpu.VMEM((tiles, HEAD, TK), BF)

    def sums(tiles):
        return pltpu.VMEM((tiles, TK, HEAD), F32)

    tail = jnp.concatenate([k[HALF:], v[HALF:]], axis=0)
    tail = lax.ppermute(tail, "dp", [(i, i + 1) for i in range(15)])
    kept = [
        pltpu.VMEM((BACK_TILES + OWN_TILES, TK, TQ), F32),
        pltpu.VMEM((BACK_TILES + OWN_TILES, 1, TQ), F32),
    ]
    packets = shape((HEADS, IN_ROWS, HEAD))
    (a,) = call(
        pack_kernel,
        "pack",
        1,
        [HBM, HBM, HBM, HBM],
        [(VMEM, packets)],
        [],
        3 * HEADS,
    )(*(pltpu.with_memory_space_constraint(each, pltpu.HBM) for each in (q, g, k, v)))
    (a,) = call(
        pack_tail_kernel,
        "pack_tail",
        1,
        [VMEM, VMEM, pl.BlockSpec(memory_space=pl.ANY)],
        [(pl.BlockSpec(memory_space=pl.ANY), packets)],
        [pltpu.VMEM((HEADS, HALF + 16, HEAD), BF)],
        1,
        input_output_aliases={2: 0},
    )(tail, starts, a)
    a = lax.all_to_all(a, "ctx", 0, 0, tiled=True)
    x = lax.ppermute(a[:, IN_X : IN_X + 192], "ctx", swap)
    st, kv, lse, delta, out, dq, keep_back, give_back, plan = call(
        forward_kernel,
        "forward",
        16,
        [SMEM, VMEM, VMEM],
        [
            (VMEM, shape((QB, 1, TQ), jnp.int32)),
            (VMEM, shape((2, 3 * MEMBERS, HALF, HEAD))),
            line,
            line,
            (VMEM, shape((MEMBERS, OUT_ROWS, HEAD))),
            wide,
            (VMEM, shape((MEMBERS, HALF, HEAD))),
            (VMEM, shape((MEMBERS, HALF, HEAD))),
            (SMEM, shape((3 * QB,), jnp.int32)),
        ],
        [turned(BACK_TILES + OWN_TILES), turned(BACK_TILES), pltpu.VMEM((HEAD, TQ), F32)]
        + kept
        + [sums(BACK_TILES), sums(BACK_TILES)],
        1,
    )(which, a, x)
    got_back = lax.ppermute(give_back, "ctx", swap)
    back = (keep_back.astype(F32) + got_back.astype(F32)).astype(BF)
    sent_back = lax.ppermute(back, "dp", [(i + 1, i) for i in range(15)])
    out, keep, *give = call(
        own_kernel,
        "own",
        11,
        [SMEM, SMEM, VMEM, VMEM, VMEM, VMEM, VMEM, VMEM, HBM, HBM],
        [
            (HBM, shape((MEMBERS, OUT_ROWS, HEAD))),
            (VMEM, shape((MEMBERS, 128, HEAD))),
        ]
        + [(VMEM, shape((2 * MEMBERS // PIECES, HALF, HEAD)))] * PIECES,
        [
            turned(BACK_TILES + OWN_TILES),
            turned(OWN_TILES),
            pltpu.VMEM((HEAD, TQ), F32),
            *kept,
            pltpu.VMEM((HEAD, TQ), F32),
            pltpu.VMEM((MEMBERS, OUT_X, HEAD), BF),
            sums(OWN_TILES),
            sums(OWN_TILES),
        ],
        QB + 1,
        input_output_aliases={8: 0},
    )(which, plan, a, kv, st, lse, delta, dq, out, back)
    got = [lax.ppermute(each, "ctx", swap) for each in give]
    (out,) = call(
        merge_kernel,
        "merge",
        1,
        [VMEM, VMEM, HBM] + [VMEM] * PIECES,
        [(HBM, shape((MEMBERS, OUT_ROWS, HEAD)))],
        [pltpu.VMEM((MEMBERS, 128, HEAD), BF)],
        1,
        input_output_aliases={2: 0},
    )(keep, sent_back, out, *got)
    out = lax.all_to_all(out, "ctx", 0, 0, tiled=True)
    attn, q_grad, k_grad, v_grad = call(
        unpack_kernel,
        "unpack",
        2,
        [VMEM],
        [(HBM, shape(q.shape)), (HBM, shape(q.shape)), (VMEM, shape(k.shape)), (VMEM, shape(k.shape))],
        [],
        2 * HEADS,
    )(out)
    return (
        attn.reshape(queries.shape),
        q_grad.reshape(queries.shape),
        k_grad.reshape(key_states.shape),
        v_grad.reshape(value_vectors.shape),
    )


def solution(mesh):
    wide = P("dp", None, "ctx", None, None)
    return jax.shard_map(
        on_device,
        mesh=mesh,
        in_specs=(wide, wide, wide, wide, P("dp", None, "ctx", None)),
        out_specs=(wide, wide, wide, wide),
        check_vma=False,
    )
```

```python
from functools import partial

import jax
import jax.numpy as jnp
from jax import lax
from jax.experimental import pallas as pl
from jax.experimental.pallas import tpu as pltpu
from jax.sharding import PartitionSpec as P

HEAD = 128
HALF = 64
MEMBERS = 16
HEADS = 16
GROUPS = 4
SPAN = 2048
BACK = 1024
TQ = 512
TK = 512
QB = SPAN // TQ
QS = TQ // HALF
KS = TK // HALF
OWN_TILES = SPAN // TK
BACK_TILES = BACK // TK
SCALE = HEAD**-0.5
FOLD = SCALE * 1.4426950408889634
NEG = -1e30
PIECES = 4
BF = jnp.bfloat16
F32 = jnp.float32

IN_Q, IN_G, IN_X, IN_S, IN_ROWS = 0, 128, 256, 448, 464
OUT_A, OUT_Q, OUT_X, OUT_ROWS = 0, 128, 256, 384

NT = (((1,), (1,)), ((), ()))
NN = (((1,), (0,)), ((), ()))


def dot(a, b, dims=NN):
    return lax.dot_general(a, b, dims, preferred_element_type=F32)


def begin(pairs, sems):
    copies = [pltpu.make_async_copy(a, b, sems.at[i]) for i, (a, b) in enumerate(pairs)]
    for c in copies:
        c.start()
    return copies


def finish(copies):
    for c in copies:
        c.wait()


def columns(n):
    return pl.ds(n * HEAD, HEAD)


def pack_kernel(q_ref, g_ref, k_ref, v_ref, s_ref, o_ref, sems):
    pairs = []
    for n in range(HEADS):
        x_ref = k_ref if n % 2 == 0 else v_ref
        pairs.append((q_ref.at[:, columns(n)], o_ref.at[n, pl.ds(IN_Q, 128)]))
        pairs.append((g_ref.at[:, columns(n)], o_ref.at[n, pl.ds(IN_G, 128)]))
        pairs.append((x_ref.at[:, columns(n // 4)], o_ref.at[n, pl.ds(IN_X, 128)]))
    copies = begin(pairs, sems)
    for n in range(HEADS):
        o_ref[n, IN_S : IN_S + 16] = s_ref[...]
    finish(copies)


def pack_tail_kernel(tail_ref, old_ref, o_ref, sems):
    del old_ref
    pairs = []
    for n in range(HEADS):
        rows = pl.ds((n % 2) * HALF, HALF)
        pairs.append((tail_ref.at[rows, columns(n // 4)], o_ref.at[n, pl.ds(IN_X + 128, HALF)]))
    finish(begin(pairs, sems))


def low_position(i):
    source = (i - QB // 2) * QS + QS - 1
    upper = (2 * MEMBERS - 1 - source) * HALF
    return BACK + jnp.where(i >= QB // 2, upper, i * TQ)


def block_of(i, st_ref, plan_ref):
    lane = lax.broadcasted_iota(jnp.int32, (1, TQ), 1)
    part = lane // HALF
    part = jnp.where(i >= QB // 2, QS - 1 - part, part)
    low = low_position(i)
    end = (low + TQ - 1) // TK + 1
    whole = (plan_ref[2 * QB + i], low)
    return st_ref[i], low + part * HALF + lane % HALF, plan_ref[QB + i], end, whole


def masked(s, start, last, base, turned, fill=NEG):
    rows = lax.broadcasted_iota(jnp.int32, (HALF, TQ), 0)
    parts = []
    for b in range(KS):
        off = base + HALF * jnp.where(turned, KS - 1 - b, b)
        seen = (rows >= start - off) & (rows <= last - off)
        parts.append(jnp.where(seen, s[b * HALF : (b + 1) * HALF], fill))
    return jnp.concatenate(parts, axis=0)


def place(t):
    upper = t >= BACK_TILES + OWN_TILES // 2
    turned = (t < BACK_TILES) | upper
    top = jnp.where(upper, 2 * BACK_TILES + OWN_TILES + OWN_TILES // 2 - 1, BACK_TILES - 1)
    return jnp.where(turned, top - t, t), turned


def packet_rows(ref, i, row):
    half = pl.ds(pl.multiple_of(row + (i // 2) * HALF, HALF), HALF)
    return ref[pl.ds((i % 2) * QS, QS), half].reshape(TQ, HEAD)


def rows_of(ref, at, count):
    return ref[pl.ds(at * count, count)].reshape(count * HALF, HEAD)


def inside(whole, t):
    return (t * TK >= whole[0]) & (t * TK + TK - 1 <= whole[1])


def softmax_tiles(lo, hi, qi, start, last, clear, kv_s, vt_s, acc_s, p_s, m_s):
    acc_s[...] = jnp.zeros_like(acc_s)

    def tile(whole, t, m, l8):
        at, turned = place(t)
        s = dot(rows_of(kv_s.at[0], at, KS), qi, NT) * FOLD
        if not whole:
            s = masked(s, start, last, t * TK, turned)
        m_new = jnp.maximum(m, jnp.max(s, axis=0, keepdims=True))
        p = jnp.exp2(s - m_new)
        p_s[t] = p
        m_s[t] = m_new
        keep = jnp.exp2(m - m_new)
        l8 = l8 * keep + jnp.sum(p.reshape(TK // 8, 8, TQ), axis=0)
        acc_s[...] = acc_s[...] * keep + dot(vt_s[at], p.astype(BF))
        return m_new, l8

    def either(t, carry):
        return lax.cond(
            inside(clear, t), partial(tile, True), partial(tile, False), t, *carry
        )

    return lax.fori_loop(
        lo, hi, either, (jnp.full((1, TQ), NEG, F32), jnp.zeros((8, TQ), F32))
    )


def grad_tile(p, at, base, qi, gi, delta, kv_s, kt_s, dk_s, dv_s, dq_s):
    dp = dot(rows_of(kv_s.at[1], at, KS), gi, NT)
    at = at - base
    ds = (p * (dp - delta)).astype(BF)
    dv_s[at] += dot(p.astype(BF), gi)
    dk_s[at] += dot(ds, qi)
    dq_s[...] += dot(kt_s[at], ds)


def grad_tiles(lo, hi, base, qi, gi, start, last, clear, lse, delta, kv_s, kt_s, dk_s, dv_s, dq_s):
    def tile(whole, t):
        at, turned = place(t)
        s = dot(rows_of(kv_s.at[0], at, KS), qi, NT) * FOLD - lse
        if not whole:
            s = masked(s, start, last, t * TK, turned)
        grad_tile(jnp.exp2(s), at, base, qi, gi, delta, kv_s, kt_s, dk_s, dv_s, dq_s)
        return 0

    def either(t, _):
        return lax.cond(inside(clear, t), partial(tile, True), partial(tile, False), t)

    lax.fori_loop(lo, hi, either, 0)


def kept_tiles(lo, hi, base, qi, gi, lse, delta, kv_s, kt_s, dk_s, dv_s, dq_s, p_s, m_s):
    def tile(t, _):
        p = p_s[t] * jnp.exp2(m_s[t] - lse)
        grad_tile(p, place(t)[0], base, qi, gi, delta, kv_s, kt_s, dk_s, dv_s, dq_s)
        return 0

    lax.fori_loop(lo, hi, tile, 0)


def forward_block(i, qi, gi, start, last, clear, first, end, kv_s, vt_s, acc_s, p_s, m_s, out_ref):
    m, l8 = softmax_tiles(first, end, qi, start, last, clear, kv_s, vt_s, acc_s, p_s, m_s)
    l = jnp.sum(l8, axis=0, keepdims=True)
    out_t = acc_s[...] * (1.0 / l)
    delta = jnp.sum(out_t * gi.astype(F32).T, axis=0, keepdims=True)
    store_block(i, OUT_A, out_t.T.astype(BF), out_ref)
    return m + jnp.log2(l), delta


def store_block(i, row, value, out_ref):
    half = pl.ds(pl.multiple_of(row + (i // 2) * HALF, HALF), HALF)
    out_ref[pl.ds((i % 2) * QS, QS), half] = value.reshape(QS, HALF, HEAD)


def block_out(i, row, o_s, out_ref, sem):
    at = (
        pl.ds((i % 2) * QS, QS),
        pl.ds(pl.multiple_of(row + (i // 2) * HALF, HALF), HALF),
    )
    return pltpu.make_async_copy(o_s.at[at], out_ref.at[at], sem)


def forward_kernel(
    core_ref, a_ref, x_ref,
    st_ref, kv_s, lse_ref, delta_ref, out_ref, dq_ref, keep_ref, give_ref, plan_ref,
    vt_s, kt_s, acc_s, p_s, m_s, dk_s, dv_s, sems,
):
    del sems
    core = core_ref[0]
    for part, row in enumerate((128, 0, HALF)):
        at = slice(part * MEMBERS, (part + 1) * MEMBERS)
        mine = a_ref[:, IN_X + row : IN_X + row + HALF]
        theirs = x_ref[:, row : row + HALF]
        kv_s[0, at] = jnp.where(core == 0, mine, theirs)
        kv_s[1, at] = jnp.where(core == 0, theirs, mine)
    for t in range(SPAN // 128):
        s0, row = (2 * t, 0) if t < 8 else (2 * t - 16, 2)
        both = a_ref[s0, IN_S : IN_S + 16].astype(F32) + a_ref[s0 + 1, IN_S : IN_S + 16].astype(F32)
        start = both[row : row + 1] * 64.0 + both[row + 1 : row + 2]
        c = (t % 4) * 128
        st_ref[t // 4, 0:1, c : c + 128] = start.astype(jnp.int32)
    for t in range(BACK_TILES + OWN_TILES):
        vt_s[t] = rows_of(kv_s.at[1], t, KS).T
    for t in range(BACK_TILES):
        kt_s[t] = rows_of(kv_s.at[0], t, KS).T
    dk_s[...] = jnp.zeros_like(dk_s)
    dv_s[...] = jnp.zeros_like(dv_s)

    spans = []
    for i in range(QB):
        first = jnp.min(st_ref[i]) // TK
        plan_ref[QB + i] = first
        plan_ref[2 * QB + i] = jnp.max(st_ref[i])
        spans.append((first, (low_position(i) + TQ - 1) // TK + 1))
    budget = core_ref[1]
    for first, end in spans:
        reach = jnp.maximum(BACK_TILES - first, 0)
        budget -= jnp.where(reach > 0, 4 * (end - first) + 5 * reach + 2, 0)
    for i, (first, end) in enumerate(spans):
        need = 4 * (end - first) + 2
        extra = (first >= BACK_TILES) & (need <= budget)
        budget -= jnp.where(extra, need, 0)
        plan_ref[i] = ((first < BACK_TILES) | extra).astype(jnp.int32)

    def q_block(i, _):
        @pl.when(plan_ref[i] == 1)
        def _():
            start, last, first, end, clear = block_of(i, st_ref, plan_ref)
            qi = packet_rows(a_ref, i, IN_Q)
            gi = packet_rows(a_ref, i, IN_G)
            lse, delta = forward_block(
                i, qi, gi, start, last, clear, first, end, kv_s, vt_s, acc_s, p_s, m_s, out_ref
            )
            lse_ref[i] = lse
            delta_ref[i] = delta
            dq_ref[i] = jnp.zeros((HEAD, TQ), F32)
            kept_tiles(
                first,
                BACK_TILES,
                0,
                qi,
                gi,
                lse,
                delta,
                kv_s,
                kt_s,
                dk_s,
                dv_s,
                dq_ref.at[i],
                p_s,
                m_s,
            )

        return 0

    lax.fori_loop(0, QB, q_block, 0)
    even = core == 0
    for t in range(BACK_TILES):
        dk, dv = dk_s[t] * SCALE, dv_s[t]
        at = slice(t * KS, (t + 1) * KS)
        keep_ref[at] = jnp.where(even, dk, dv).astype(BF).reshape(KS, HALF, HEAD)
        give_ref[at] = jnp.where(even, dv, dk).astype(BF).reshape(KS, HALF, HEAD)


def own_kernel(
    core_ref, plan_ref, a_ref, kv_ref, st_ref, lse_ref, delta_ref, dq_ref, old_ref, after_ref,
    out_ref, keep_ref, *rest,
):
    del old_ref, after_ref
    give_refs, rest = rest[:PIECES], rest[PIECES:]
    vt_s, kt_s, acc_s, p_s, m_s, dq_s, o_s, dk_s, dv_s, sems = rest
    core = core_ref[0]
    dk_s[...] = jnp.zeros_like(dk_s)
    dv_s[...] = jnp.zeros_like(dv_s)
    for t in range(OWN_TILES):
        kt_s[t] = rows_of(kv_ref.at[0], BACK_TILES + t, KS).T
        vt_s[BACK_TILES + t] = rows_of(kv_ref.at[1], BACK_TILES + t, KS).T

    def q_block(i, _):
        qi = packet_rows(a_ref, i, IN_Q)
        gi = packet_rows(a_ref, i, IN_G)
        start, last, first, end, clear = block_of(i, st_ref, plan_ref)

        low = jnp.maximum(first, BACK_TILES)

        @pl.when(plan_ref[i] == 0)
        def _():
            lse, delta = forward_block(
                i, qi, gi, start, last, clear, first, end, kv_ref, vt_s, acc_s, p_s, m_s, o_s
            )
            dq_s[...] = jnp.zeros_like(dq_s)
            kept_tiles(
                low,
                end,
                BACK_TILES,
                qi,
                gi,
                lse,
                delta,
                kv_ref,
                kt_s,
                dk_s,
                dv_s,
                dq_s,
                p_s,
                m_s,
            )

        @pl.when(plan_ref[i] == 1)
        def _():
            dq_s[...] = dq_ref[i]
            grad_tiles(
                low,
                end,
                BACK_TILES,
                qi,
                gi,
                start,
                last,
                clear,
                lse_ref[i],
                delta_ref[i],
                kv_ref,
                kt_s,
                dk_s,
                dv_s,
                dq_s,
            )

        store_block(i, OUT_Q, (dq_s[...] * SCALE).T.astype(BF), o_s)
        block_out(i, OUT_Q, o_s, out_ref, sems.at[i]).start()

        @pl.when(plan_ref[i] == 0)
        def _():
            copy = block_out(i, OUT_A, o_s, out_ref, sems.at[QB])
            copy.start()
            copy.wait()

        return 0

    lax.fori_loop(0, QB, q_block, 0)
    for i in range(QB):
        block_out(i, OUT_Q, o_s, out_ref, sems.at[i]).wait()
    even = core == 0
    for t in range(OWN_TILES):
        dk, dv = dk_s[t] * SCALE, dv_s[t]
        half, s0 = t // (OWN_TILES // 2), (t % (OWN_TILES // 2)) * KS
        at = (slice(s0, s0 + KS), slice(half * HALF, half * HALF + HALF))
        keep_ref[at] = jnp.where(even, dk, dv).astype(BF).reshape(KS, HALF, HEAD)
        given = jnp.where(even, dv, dk).astype(BF).reshape(KS, HALF, HEAD)
        for b in range(KS):
            piece, row = divmod(t * KS + b, 2 * MEMBERS // PIECES)
            give_refs[piece][row] = given[b]


def tie_kernel(x_ref, after_ref, o_ref, sems):
    del x_ref, after_ref, o_ref, sems


def merge_kernel(keep_ref, old_ref, *rest):
    del old_ref
    got_refs, (out_ref, upper_ref, x_s, sems) = rest[:PIECES], rest[PIECES:]
    count = 2 * MEMBERS // PIECES
    for piece, got_ref in enumerate(got_refs):
        half, s0 = divmod(piece * count, MEMBERS)
        at = (slice(s0, s0 + count), slice(half * HALF, half * HALF + HALF))
        total = keep_ref[at].astype(F32) + got_ref[...].astype(F32)
        if half == 0:
            x_s[s0 : s0 + count] = total.astype(BF)
        else:
            upper_ref[s0 : s0 + count] = total
    finish(begin([(x_s, out_ref.at[:, pl.ds(OUT_X, HALF)])], sems))


def merge_back_kernel(upper_ref, back_ref, old_ref, out_ref, x_s, sems):
    del old_ref
    x_s[...] = (upper_ref[...] + back_ref[...].astype(F32)).astype(BF)
    finish(begin([(x_s, out_ref.at[:, pl.ds(OUT_X + HALF, HALF)])], sems))


def unpack_kernel(t_ref, a_ref, q_ref, k_ref, v_ref, k_s, v_s, sems):
    pairs = []
    for n in range(HEADS):
        pairs.append((t_ref.at[n, pl.ds(OUT_A, 128)], a_ref.at[:, columns(n)]))
        pairs.append((t_ref.at[n, pl.ds(OUT_Q, 128)], q_ref.at[:, columns(n)]))
    copies = begin(pairs, sems)
    for index, (n0, o_s, o_ref) in enumerate(((0, k_s, k_ref), (1, v_s, v_ref))):
        for g in range(GROUPS):
            n = 4 * g + n0
            total = t_ref[n, OUT_X : OUT_X + 128].astype(F32) + t_ref[
                n + 2, OUT_X : OUT_X + 128
            ].astype(F32)
            o_s[:, g * HEAD : (g + 1) * HEAD] = total.astype(BF)
        copies.append(pltpu.make_async_copy(o_s, o_ref, sems.at[2 * HEADS + index]))
        copies[-1].start()
    finish(copies)


def shape(dims, dtype=BF):
    return jax.ShapeDtypeStruct(dims, dtype)


HBM = pl.BlockSpec(memory_space=pltpu.HBM)
VMEM = pl.BlockSpec(memory_space=pltpu.VMEM)
SMEM = pl.BlockSpec(memory_space=pltpu.SMEM)


def call(kernel, name, us, ins, outs, scratch, copies, mib=32, **more):
    return pl.pallas_call(
        kernel,
        in_specs=ins,
        out_specs=[space for space, _ in outs],
        out_shape=[what for _, what in outs],
        scratch_shapes=scratch + [pltpu.SemaphoreType.DMA((copies,))],
        compiler_params=pltpu.CompilerParams(vmem_limit_bytes=mib * 1024 * 1024),
        cost_estimate=pl.CostEstimate(
            flops=int(us * 4e8), bytes_accessed=1 << 20, transcendentals=0
        ),
        name=name,
        **more,
    )


def tie(x, after):
    (x,) = call(
        tie_kernel,
        "tie",
        1,
        [HBM, HBM],
        [(HBM, shape(x.shape))],
        [],
        1,
        input_output_aliases={0: 0},
    )(x, after)
    return x


def on_device(queries, key_states, value_vectors, grad_out, doc_start):
    cycle = lax.axis_index("dp")
    core = lax.axis_index("ctx") % 2
    q = queries.reshape(128, HEADS * HEAD)
    g = grad_out.reshape(128, HEADS * HEAD)
    k = key_states.reshape(128, GROUPS * HEAD)
    v = value_vectors.reshape(128, GROUPS * HEAD)
    swap = [(i, i ^ 1) for i in range(MEMBERS)]
    budget = jnp.where(cycle % 4 == 0, 0, jnp.where(cycle % 4 == 1, 64, 40))
    which = jnp.stack([core, budget])

    rel = doc_start.reshape(2, HALF) - (cycle * SPAN - BACK)
    parts = jnp.stack([rel // 64, rel % 64], axis=1).reshape(4, HALF).astype(BF)
    zero = jnp.zeros_like(parts)
    starts = jnp.where(
        core == 0,
        jnp.concatenate([parts, zero], axis=1),
        jnp.concatenate([zero, parts], axis=1),
    )
    starts = jnp.pad(starts, ((0, 12), (0, 0)))

    wide = (VMEM, shape((QB, HEAD, TQ), F32))
    line = (VMEM, shape((QB, 1, TQ), F32))

    def turned(tiles):
        return pltpu.VMEM((tiles, HEAD, TK), BF)

    def sums(tiles):
        return pltpu.VMEM((tiles, TK, HEAD), F32)

    tail = jnp.concatenate([k[HALF:], v[HALF:]], axis=0)
    tail = lax.ppermute(tail, "dp", [(i, i + 1) for i in range(15)])
    kept = [
        pltpu.VMEM((BACK_TILES + OWN_TILES, TK, TQ), F32),
        pltpu.VMEM((BACK_TILES + OWN_TILES, 1, TQ), F32),
    ]
    packets = shape((HEADS, IN_ROWS, HEAD))
    (a,) = call(
        pack_kernel,
        "pack",
        1,
        [HBM, HBM, HBM, HBM, VMEM],
        [(VMEM, packets)],
        [],
        3 * HEADS,
    )(*(pltpu.with_memory_space_constraint(each, pltpu.HBM) for each in (q, g, k, v)), starts)
    (a,) = call(
        pack_tail_kernel,
        "pack_tail",
        1,
        [VMEM, pl.BlockSpec(memory_space=pl.ANY)],
        [(pl.BlockSpec(memory_space=pl.ANY), packets)],
        [],
        HEADS,
        input_output_aliases={1: 0},
    )(tail, a)
    a = lax.all_to_all(a, "ctx", 0, 0, tiled=True)
    x = lax.ppermute(a[:, IN_X : IN_X + 192], "ctx", swap)
    st, kv, lse, delta, out, dq, keep_back, give_back, plan = call(
        forward_kernel,
        "forward",
        16,
        [SMEM, VMEM, VMEM],
        [
            (VMEM, shape((QB, 1, TQ), jnp.int32)),
            (VMEM, shape((2, 3 * MEMBERS, HALF, HEAD))),
            line,
            line,
            (VMEM, shape((MEMBERS, OUT_ROWS, HEAD))),
            wide,
            (VMEM, shape((MEMBERS, HALF, HEAD))),
            (VMEM, shape((MEMBERS, HALF, HEAD))),
            (SMEM, shape((3 * QB,), jnp.int32)),
        ],
        [turned(BACK_TILES + OWN_TILES), turned(BACK_TILES), pltpu.VMEM((HEAD, TQ), F32)]
        + kept
        + [sums(BACK_TILES), sums(BACK_TILES)],
        1,
    )(which, a, x)
    got_back = lax.ppermute(give_back, "ctx", swap)
    back = (keep_back.astype(F32) + got_back.astype(F32)).astype(BF)
    sent_back = lax.ppermute(back, "dp", [(i + 1, i) for i in range(15)])
    out, keep, *give = call(
        own_kernel,
        "own",
        11,
        [SMEM, SMEM, VMEM, VMEM, VMEM, VMEM, VMEM, VMEM, HBM, HBM],
        [
            (HBM, shape((MEMBERS, OUT_ROWS, HEAD))),
            (VMEM, shape((MEMBERS, 128, HEAD))),
        ]
        + [(VMEM, shape((2 * MEMBERS // PIECES, HALF, HEAD)))] * PIECES,
        [
            turned(BACK_TILES + OWN_TILES),
            turned(OWN_TILES),
            pltpu.VMEM((HEAD, TQ), F32),
            *kept,
            pltpu.VMEM((HEAD, TQ), F32),
            pltpu.VMEM((MEMBERS, OUT_X, HEAD), BF),
            sums(OWN_TILES),
            sums(OWN_TILES),
        ],
        QB + 1,
        input_output_aliases={8: 0},
    )(which, plan, a, kv, st, lse, delta, dq, out, back)
    got = [lax.ppermute(each, "ctx", swap) for each in give]
    out, upper = call(
        merge_kernel,
        "merge",
        1,
        [VMEM, HBM] + [VMEM] * PIECES,
        [(HBM, shape((MEMBERS, OUT_ROWS, HEAD))), (VMEM, shape((MEMBERS, HALF, HEAD), F32))],
        [pltpu.VMEM((MEMBERS, HALF, HEAD), BF)],
        1,
        input_output_aliases={1: 0},
    )(keep, out, *got)
    (out,) = call(
        merge_back_kernel,
        "merge_back",
        1,
        [VMEM, VMEM, HBM],
        [(HBM, shape((MEMBERS, OUT_ROWS, HEAD)))],
        [pltpu.VMEM((MEMBERS, HALF, HEAD), BF)],
        1,
        input_output_aliases={2: 0},
    )(upper, sent_back, out)
    out = lax.all_to_all(out, "ctx", 0, 0, tiled=True)
    attn, q_grad, k_grad, v_grad = call(
        unpack_kernel,
        "unpack",
        2,
        [VMEM],
        [(HBM, shape(q.shape)), (HBM, shape(q.shape)), (HBM, shape(k.shape)), (HBM, shape(k.shape))],
        [pltpu.VMEM(k.shape, BF), pltpu.VMEM(k.shape, BF)],
        2 * HEADS + 2,
    )(out)
    return (
        attn.reshape(queries.shape),
        q_grad.reshape(queries.shape),
        k_grad.reshape(key_states.shape),
        v_grad.reshape(value_vectors.shape),
    )


def solution(mesh):
    wide = P("dp", None, "ctx", None, None)
    return jax.shard_map(
        on_device,
        mesh=mesh,
        in_specs=(wide, wide, wide, wide, P("dp", None, "ctx", None)),
        out_specs=(wide, wide, wide, wide),
        check_vma=False,
    )
```

```python
from functools import partial

import jax
import jax.numpy as jnp
from jax import lax
from jax.experimental import pallas as pl
from jax.experimental.pallas import tpu as pltpu
from jax.sharding import PartitionSpec as P

HEAD = 128
HALF = 64
MEMBERS = 16
HEADS = 16
GROUPS = 4
SPAN = 2048
BACK = 1024
TQ = 512
TK = 512
QB = SPAN // TQ
QS = TQ // HALF
KS = TK // HALF
OWN_TILES = SPAN // TK
BACK_TILES = BACK // TK
SCALE = HEAD**-0.5
FOLD = SCALE * 1.4426950408889634
NEG = -1e30
PIECES = 4
BF = jnp.bfloat16
F32 = jnp.float32

IN_Q, IN_G, IN_X, IN_S, IN_ROWS = 0, 128, 256, 448, 464
OUT_A, OUT_Q, OUT_X, OUT_ROWS = 0, 128, 256, 384

NT = (((1,), (1,)), ((), ()))
NN = (((1,), (0,)), ((), ()))


def dot(a, b, dims=NN):
    return lax.dot_general(a, b, dims, preferred_element_type=F32)


def begin(pairs, sems):
    copies = [pltpu.make_async_copy(a, b, sems.at[i]) for i, (a, b) in enumerate(pairs)]
    for c in copies:
        c.start()
    return copies


def finish(copies):
    for c in copies:
        c.wait()


def columns(n):
    return pl.ds(n * HEAD, HEAD)


def pack_kernel(q_ref, g_ref, k_ref, v_ref, s_ref, o_ref, sems):
    pairs = []
    for n in range(HEADS):
        x_ref = k_ref if n % 2 == 0 else v_ref
        pairs.append((q_ref.at[:, columns(n)], o_ref.at[n, pl.ds(IN_Q, 128)]))
        pairs.append((g_ref.at[:, columns(n)], o_ref.at[n, pl.ds(IN_G, 128)]))
        pairs.append((x_ref.at[:, columns(n // 4)], o_ref.at[n, pl.ds(IN_X, 128)]))
    copies = begin(pairs, sems)
    for n in range(HEADS):
        o_ref[n, IN_S : IN_S + 16] = s_ref[...]
    finish(copies)


def pack_tail_kernel(tail_ref, old_ref, o_ref, sems):
    del old_ref
    pairs = []
    for n in range(HEADS):
        rows = pl.ds((n % 2) * HALF, HALF)
        pairs.append((tail_ref.at[rows, columns(n // 4)], o_ref.at[n, pl.ds(IN_X + 128, HALF)]))
    finish(begin(pairs, sems))


def low_position(i):
    source = (i - QB // 2) * QS + QS - 1
    upper = (2 * MEMBERS - 1 - source) * HALF
    return BACK + jnp.where(i >= QB // 2, upper, i * TQ)


def block_of(i, st_ref, plan_ref):
    lane = lax.broadcasted_iota(jnp.int32, (1, TQ), 1)
    part = lane // HALF
    part = jnp.where(i >= QB // 2, QS - 1 - part, part)
    low = low_position(i)
    end = (low + TQ - 1) // TK + 1
    whole = (plan_ref[2 * QB + i], low)
    return st_ref[i], low + part * HALF + lane % HALF, plan_ref[QB + i], end, whole


def masked(s, start, last, base, turned, fill=NEG):
    rows = lax.broadcasted_iota(jnp.int32, (HALF, TQ), 0)
    parts = []
    for b in range(KS):
        off = base + HALF * jnp.where(turned, KS - 1 - b, b)
        seen = (rows >= start - off) & (rows <= last - off)
        parts.append(jnp.where(seen, s[b * HALF : (b + 1) * HALF], fill))
    return jnp.concatenate(parts, axis=0)


def place(t):
    upper = t >= BACK_TILES + OWN_TILES // 2
    turned = (t < BACK_TILES) | upper
    top = jnp.where(upper, 2 * BACK_TILES + OWN_TILES + OWN_TILES // 2 - 1, BACK_TILES - 1)
    return jnp.where(turned, top - t, t), turned


def packet_rows(ref, i, row):
    half = pl.ds(pl.multiple_of(row + (i // 2) * HALF, HALF), HALF)
    return ref[pl.ds((i % 2) * QS, QS), half].reshape(TQ, HEAD)


def rows_of(ref, at, count):
    return ref[pl.ds(at * count, count)].reshape(count * HALF, HEAD)


def inside(whole, t):
    return (t * TK >= whole[0]) & (t * TK + TK - 1 <= whole[1])


def softmax_tiles(lo, hi, qi, start, last, clear, kv_s, vt_s, acc_s, p_s, m_s):
    acc_s[...] = jnp.zeros_like(acc_s)

    def tile(whole, t, m, l8):
        at, turned = place(t)
        s = dot(rows_of(kv_s.at[0], at, KS), qi, NT) * FOLD
        if not whole:
            s = masked(s, start, last, t * TK, turned)
        m_new = jnp.maximum(m, jnp.max(s, axis=0, keepdims=True))
        p = jnp.exp2(s - m_new)
        p_s[t] = p
        m_s[t] = m_new
        keep = jnp.exp2(m - m_new)
        l8 = l8 * keep + jnp.sum(p.reshape(TK // 8, 8, TQ), axis=0)
        acc_s[...] = acc_s[...] * keep + dot(vt_s[at], p.astype(BF))
        return m_new, l8

    def either(t, carry):
        return lax.cond(
            inside(clear, t), partial(tile, True), partial(tile, False), t, *carry
        )

    return lax.fori_loop(
        lo, hi, either, (jnp.full((1, TQ), NEG, F32), jnp.zeros((8, TQ), F32))
    )


def grad_tile(p, at, base, qi, gi, delta, kv_s, kt_s, dk_s, dv_s, dq_s):
    dp = dot(rows_of(kv_s.at[1], at, KS), gi, NT)
    at = at - base
    ds = (p * (dp - delta)).astype(BF)
    dv_s[at] += dot(p.astype(BF), gi)
    dk_s[at] += dot(ds, qi)
    dq_s[...] += dot(kt_s[at], ds)


def grad_tiles(lo, hi, base, qi, gi, start, last, clear, lse, delta, kv_s, kt_s, dk_s, dv_s, dq_s):
    def tile(whole, t):
        at, turned = place(t)
        s = dot(rows_of(kv_s.at[0], at, KS), qi, NT) * FOLD - lse
        if not whole:
            s = masked(s, start, last, t * TK, turned)
        grad_tile(jnp.exp2(s), at, base, qi, gi, delta, kv_s, kt_s, dk_s, dv_s, dq_s)
        return 0

    def either(t, _):
        return lax.cond(inside(clear, t), partial(tile, True), partial(tile, False), t)

    lax.fori_loop(lo, hi, either, 0)


def kept_tiles(lo, hi, base, qi, gi, lse, delta, kv_s, kt_s, dk_s, dv_s, dq_s, p_s, m_s):
    def tile(t, _):
        p = p_s[t] * jnp.exp2(m_s[t] - lse)
        grad_tile(p, place(t)[0], base, qi, gi, delta, kv_s, kt_s, dk_s, dv_s, dq_s)
        return 0

    lax.fori_loop(lo, hi, tile, 0)


def forward_block(i, qi, gi, start, last, clear, first, end, kv_s, vt_s, acc_s, p_s, m_s, out_ref):
    m, l8 = softmax_tiles(first, end, qi, start, last, clear, kv_s, vt_s, acc_s, p_s, m_s)
    l = jnp.sum(l8, axis=0, keepdims=True)
    out_t = acc_s[...] * (1.0 / l)
    delta = jnp.sum(out_t * gi.astype(F32).T, axis=0, keepdims=True)
    store_block(i, OUT_A, out_t.T.astype(BF), out_ref)
    return m + jnp.log2(l), delta


def store_block(i, row, value, out_ref):
    half = pl.ds(pl.multiple_of(row + (i // 2) * HALF, HALF), HALF)
    out_ref[pl.ds((i % 2) * QS, QS), half] = value.reshape(QS, HALF, HEAD)


def block_out(i, row, o_s, out_ref, sem):
    at = (
        pl.ds((i % 2) * QS, QS),
        pl.ds(pl.multiple_of(row + (i // 2) * HALF, HALF), HALF),
    )
    return pltpu.make_async_copy(o_s.at[at], out_ref.at[at], sem)


def forward_kernel(
    core_ref, a_ref, x_ref,
    st_ref, kv_s, lse_ref, delta_ref, out_ref, dq_ref, keep_ref, give_ref, plan_ref,
    vt_s, kt_s, acc_s, p_s, m_s, dk_s, dv_s, sems,
):
    del sems
    core = core_ref[0]
    for part, row in enumerate((128, 0, HALF)):
        at = slice(part * MEMBERS, (part + 1) * MEMBERS)
        mine = a_ref[:, IN_X + row : IN_X + row + HALF]
        theirs = x_ref[:, row : row + HALF]
        kv_s[0, at] = jnp.where(core == 0, mine, theirs)
        kv_s[1, at] = jnp.where(core == 0, theirs, mine)
    for t in range(SPAN // 128):
        s0, row = (2 * t, 0) if t < 8 else (2 * t - 16, 2)
        both = a_ref[s0, IN_S : IN_S + 16].astype(F32) + a_ref[s0 + 1, IN_S : IN_S + 16].astype(F32)
        start = both[row : row + 1] * 64.0 + both[row + 1 : row + 2]
        c = (t % 4) * 128
        st_ref[t // 4, 0:1, c : c + 128] = start.astype(jnp.int32)
    lower = BACK_TILES + OWN_TILES // 2
    for t in range(lower):
        vt_s[t] = rows_of(kv_s.at[1], t, KS).T
    for t in range(BACK_TILES):
        kt_s[t] = rows_of(kv_s.at[0], t, KS).T
    dk_s[...] = jnp.zeros_like(dk_s)
    dv_s[...] = jnp.zeros_like(dv_s)

    spans = []
    for i in range(QB):
        first = jnp.min(st_ref[i]) // TK
        plan_ref[QB + i] = first
        plan_ref[2 * QB + i] = jnp.max(st_ref[i])
        spans.append((first, (low_position(i) + TQ - 1) // TK + 1))
    budget = core_ref[1]
    for first, end in spans:
        reach = jnp.maximum(BACK_TILES - first, 0)
        budget -= jnp.where(reach > 0, 4 * (end - first) + 5 * reach + 2, 0)
    for i, (first, end) in enumerate(spans):
        need = 4 * (end - first) + 2
        extra = (first >= BACK_TILES) & (need <= budget)
        budget -= jnp.where(extra, need, 0)
        plan_ref[i] = ((first < BACK_TILES) | extra).astype(jnp.int32)

    @pl.when(plan_ref[QB // 2] + plan_ref[QB // 2 + 1] > 0)
    def _():
        for t in range(lower, BACK_TILES + OWN_TILES):
            vt_s[t] = rows_of(kv_s.at[1], t, KS).T

    def q_block(i, _):
        @pl.when(plan_ref[i] == 1)
        def _():
            start, last, first, end, clear = block_of(i, st_ref, plan_ref)
            qi = packet_rows(a_ref, i, IN_Q)
            gi = packet_rows(a_ref, i, IN_G)
            lse, delta = forward_block(
                i, qi, gi, start, last, clear, first, end, kv_s, vt_s, acc_s, p_s, m_s, out_ref
            )
            lse_ref[i] = lse
            delta_ref[i] = delta
            dq_ref[i] = jnp.zeros((HEAD, TQ), F32)
            kept_tiles(
                first,
                BACK_TILES,
                0,
                qi,
                gi,
                lse,
                delta,
                kv_s,
                kt_s,
                dk_s,
                dv_s,
                dq_ref.at[i],
                p_s,
                m_s,
            )

        return 0

    lax.fori_loop(0, QB, q_block, 0)
    even = core == 0
    for t in range(BACK_TILES):
        dk, dv = dk_s[t] * SCALE, dv_s[t]
        at = slice(t * KS, (t + 1) * KS)
        keep_ref[at] = jnp.where(even, dk, dv).astype(BF).reshape(KS, HALF, HEAD)
        give_ref[at] = jnp.where(even, dv, dk).astype(BF).reshape(KS, HALF, HEAD)


def own_kernel(
    core_ref, plan_ref, a_ref, kv_ref, st_ref, lse_ref, delta_ref, dq_ref, old_ref, after_ref,
    out_ref, keep_ref, *rest,
):
    del old_ref, after_ref
    give_refs, rest = rest[:PIECES], rest[PIECES:]
    vt_s, kt_s, acc_s, p_s, m_s, dq_s, o_s, dk_s, dv_s, sems = rest
    core = core_ref[0]
    dk_s[...] = jnp.zeros_like(dk_s)
    dv_s[...] = jnp.zeros_like(dv_s)
    for t in range(OWN_TILES):
        kt_s[t] = rows_of(kv_ref.at[0], BACK_TILES + t, KS).T
        vt_s[BACK_TILES + t] = rows_of(kv_ref.at[1], BACK_TILES + t, KS).T

    def q_block(i, _):
        qi = packet_rows(a_ref, i, IN_Q)
        gi = packet_rows(a_ref, i, IN_G)
        start, last, first, end, clear = block_of(i, st_ref, plan_ref)

        low = jnp.maximum(first, BACK_TILES)

        @pl.when(plan_ref[i] == 0)
        def _():
            lse, delta = forward_block(
                i, qi, gi, start, last, clear, first, end, kv_ref, vt_s, acc_s, p_s, m_s, o_s
            )
            dq_s[...] = jnp.zeros_like(dq_s)
            kept_tiles(
                low,
                end,
                BACK_TILES,
                qi,
                gi,
                lse,
                delta,
                kv_ref,
                kt_s,
                dk_s,
                dv_s,
                dq_s,
                p_s,
                m_s,
            )

        @pl.when(plan_ref[i] == 1)
        def _():
            dq_s[...] = dq_ref[i]
            grad_tiles(
                low,
                end,
                BACK_TILES,
                qi,
                gi,
                start,
                last,
                clear,
                lse_ref[i],
                delta_ref[i],
                kv_ref,
                kt_s,
                dk_s,
                dv_s,
                dq_s,
            )

        store_block(i, OUT_Q, (dq_s[...] * SCALE).T.astype(BF), o_s)
        block_out(i, OUT_Q, o_s, out_ref, sems.at[i]).start()

        @pl.when(plan_ref[i] == 0)
        def _():
            copy = block_out(i, OUT_A, o_s, out_ref, sems.at[QB])
            copy.start()
            copy.wait()

        return 0

    lax.fori_loop(0, QB, q_block, 0)
    for i in range(QB):
        block_out(i, OUT_Q, o_s, out_ref, sems.at[i]).wait()
    even = core == 0
    for t in range(OWN_TILES):
        dk, dv = dk_s[t] * SCALE, dv_s[t]
        half, s0 = t // (OWN_TILES // 2), (t % (OWN_TILES // 2)) * KS
        at = (slice(s0, s0 + KS), slice(half * HALF, half * HALF + HALF))
        keep_ref[at] = jnp.where(even, dk, dv).astype(BF).reshape(KS, HALF, HEAD)
        given = jnp.where(even, dv, dk).astype(BF).reshape(KS, HALF, HEAD)
        for b in range(KS):
            piece, row = divmod(t * KS + b, 2 * MEMBERS // PIECES)
            give_refs[piece][row] = given[b]


def tie_kernel(x_ref, after_ref, o_ref, sems):
    del x_ref, after_ref, o_ref, sems


def merge_kernel(keep_ref, old_ref, *rest):
    del old_ref
    got_refs, (out_ref, upper_ref, x_s, sems) = rest[:PIECES], rest[PIECES:]
    count = 2 * MEMBERS // PIECES
    for piece, got_ref in enumerate(got_refs):
        half, s0 = divmod(piece * count, MEMBERS)
        at = (slice(s0, s0 + count), slice(half * HALF, half * HALF + HALF))
        total = keep_ref[at].astype(F32) + got_ref[...].astype(F32)
        if half == 0:
            x_s[s0 : s0 + count] = total.astype(BF)
        else:
            upper_ref[s0 : s0 + count] = total
    finish(begin([(x_s, out_ref.at[:, pl.ds(OUT_X, HALF)])], sems))


def merge_back_kernel(upper_ref, back_ref, old_ref, out_ref, x_s, sems):
    del old_ref
    x_s[...] = (upper_ref[...] + back_ref[...].astype(F32)).astype(BF)
    finish(begin([(x_s, out_ref.at[:, pl.ds(OUT_X + HALF, HALF)])], sems))


def unpack_kernel(t_ref, a_ref, q_ref, k_ref, v_ref, k_s, v_s, sems):
    pairs = []
    for n in range(HEADS):
        pairs.append((t_ref.at[n, pl.ds(OUT_A, 128)], a_ref.at[:, columns(n)]))
        pairs.append((t_ref.at[n, pl.ds(OUT_Q, 128)], q_ref.at[:, columns(n)]))
    copies = begin(pairs, sems)
    for index, (n0, o_s, o_ref) in enumerate(((0, k_s, k_ref), (1, v_s, v_ref))):
        for g in range(GROUPS):
            n = 4 * g + n0
            total = t_ref[n, OUT_X : OUT_X + 128].astype(F32) + t_ref[
                n + 2, OUT_X : OUT_X + 128
            ].astype(F32)
            o_s[:, g * HEAD : (g + 1) * HEAD] = total.astype(BF)
        copies.append(pltpu.make_async_copy(o_s, o_ref, sems.at[2 * HEADS + index]))
        copies[-1].start()
    finish(copies)


def shape(dims, dtype=BF):
    return jax.ShapeDtypeStruct(dims, dtype)


HBM = pl.BlockSpec(memory_space=pltpu.HBM)
VMEM = pl.BlockSpec(memory_space=pltpu.VMEM)
SMEM = pl.BlockSpec(memory_space=pltpu.SMEM)


def call(kernel, name, us, ins, outs, scratch, copies, mib=32, **more):
    return pl.pallas_call(
        kernel,
        in_specs=ins,
        out_specs=[space for space, _ in outs],
        out_shape=[what for _, what in outs],
        scratch_shapes=scratch + [pltpu.SemaphoreType.DMA((copies,))],
        compiler_params=pltpu.CompilerParams(vmem_limit_bytes=mib * 1024 * 1024),
        cost_estimate=pl.CostEstimate(
            flops=int(us * 4e8), bytes_accessed=1 << 20, transcendentals=0
        ),
        name=name,
        **more,
    )


def tie(x, after):
    (x,) = call(
        tie_kernel,
        "tie",
        1,
        [HBM, HBM],
        [(HBM, shape(x.shape))],
        [],
        1,
        input_output_aliases={0: 0},
    )(x, after)
    return x


def on_device(queries, key_states, value_vectors, grad_out, doc_start):
    cycle = lax.axis_index("dp")
    core = lax.axis_index("ctx") % 2
    q = queries.reshape(128, HEADS * HEAD)
    g = grad_out.reshape(128, HEADS * HEAD)
    k = key_states.reshape(128, GROUPS * HEAD)
    v = value_vectors.reshape(128, GROUPS * HEAD)
    swap = [(i, i ^ 1) for i in range(MEMBERS)]
    budget = jnp.where(cycle % 4 == 0, 0, jnp.where(cycle % 4 == 3, 16, 56))
    which = jnp.stack([core, budget])

    rel = doc_start.reshape(2, HALF) - (cycle * SPAN - BACK)
    parts = jnp.stack([rel // 64, rel % 64], axis=1).reshape(4, HALF).astype(BF)
    zero = jnp.zeros_like(parts)
    starts = jnp.where(
        core == 0,
        jnp.concatenate([parts, zero], axis=1),
        jnp.concatenate([zero, parts], axis=1),
    )
    starts = jnp.pad(starts, ((0, 12), (0, 0)))

    wide = (VMEM, shape((QB, HEAD, TQ), F32))
    line = (VMEM, shape((QB, 1, TQ), F32))

    def turned(tiles):
        return pltpu.VMEM((tiles, HEAD, TK), BF)

    def sums(tiles):
        return pltpu.VMEM((tiles, TK, HEAD), F32)

    tail = jnp.concatenate([k[HALF:], v[HALF:]], axis=0)
    tail = lax.ppermute(tail, "dp", [(i, i + 1) for i in range(15)])
    kept = [
        pltpu.VMEM((BACK_TILES + OWN_TILES, TK, TQ), F32),
        pltpu.VMEM((BACK_TILES + OWN_TILES, 1, TQ), F32),
    ]
    packets = shape((HEADS, IN_ROWS, HEAD))
    (a,) = call(
        pack_kernel,
        "pack",
        1,
        [HBM, HBM, HBM, HBM, VMEM],
        [(VMEM, packets)],
        [],
        3 * HEADS,
    )(*(pltpu.with_memory_space_constraint(each, pltpu.HBM) for each in (q, g, k, v)), starts)
    (a,) = call(
        pack_tail_kernel,
        "pack_tail",
        1,
        [VMEM, pl.BlockSpec(memory_space=pl.ANY)],
        [(pl.BlockSpec(memory_space=pl.ANY), packets)],
        [],
        HEADS,
        input_output_aliases={1: 0},
    )(tail, a)
    a = lax.all_to_all(a, "ctx", 0, 0, tiled=True)
    x = lax.ppermute(a[:, IN_X : IN_X + 192], "ctx", swap)
    st, kv, lse, delta, out, dq, keep_back, give_back, plan = call(
        forward_kernel,
        "forward",
        16,
        [SMEM, VMEM, VMEM],
        [
            (VMEM, shape((QB, 1, TQ), jnp.int32)),
            (VMEM, shape((2, 3 * MEMBERS, HALF, HEAD))),
            line,
            line,
            (VMEM, shape((MEMBERS, OUT_ROWS, HEAD))),
            wide,
            (VMEM, shape((MEMBERS, HALF, HEAD))),
            (VMEM, shape((MEMBERS, HALF, HEAD))),
            (SMEM, shape((3 * QB,), jnp.int32)),
        ],
        [turned(BACK_TILES + OWN_TILES), turned(BACK_TILES), pltpu.VMEM((HEAD, TQ), F32)]
        + kept
        + [sums(BACK_TILES), sums(BACK_TILES)],
        1,
    )(which, a, x)
    got_back = lax.ppermute(give_back, "ctx", swap)
    back = (keep_back.astype(F32) + got_back.astype(F32)).astype(BF)
    sent_back = lax.ppermute(back, "dp", [(i + 1, i) for i in range(15)])
    out, keep, *give = call(
        own_kernel,
        "own",
        11,
        [SMEM, SMEM, VMEM, VMEM, VMEM, VMEM, VMEM, VMEM, HBM, HBM],
        [
            (HBM, shape((MEMBERS, OUT_ROWS, HEAD))),
            (VMEM, shape((MEMBERS, 128, HEAD))),
        ]
        + [(VMEM, shape((2 * MEMBERS // PIECES, HALF, HEAD)))] * PIECES,
        [
            turned(BACK_TILES + OWN_TILES),
            turned(OWN_TILES),
            pltpu.VMEM((HEAD, TQ), F32),
            *kept,
            pltpu.VMEM((HEAD, TQ), F32),
            pltpu.VMEM((MEMBERS, OUT_X, HEAD), BF),
            sums(OWN_TILES),
            sums(OWN_TILES),
        ],
        QB + 1,
        input_output_aliases={8: 0},
    )(which, plan, a, kv, st, lse, delta, dq, out, back)
    got = [lax.ppermute(each, "ctx", swap) for each in give]
    out, upper = call(
        merge_kernel,
        "merge",
        1,
        [VMEM, HBM] + [VMEM] * PIECES,
        [(HBM, shape((MEMBERS, OUT_ROWS, HEAD))), (VMEM, shape((MEMBERS, HALF, HEAD), F32))],
        [pltpu.VMEM((MEMBERS, HALF, HEAD), BF)],
        1,
        input_output_aliases={1: 0},
    )(keep, out, *got)
    (out,) = call(
        merge_back_kernel,
        "merge_back",
        1,
        [VMEM, VMEM, HBM],
        [(HBM, shape((MEMBERS, OUT_ROWS, HEAD)))],
        [pltpu.VMEM((MEMBERS, HALF, HEAD), BF)],
        1,
        input_output_aliases={2: 0},
    )(upper, sent_back, out)
    out = lax.all_to_all(out, "ctx", 0, 0, tiled=True)
    attn, q_grad, k_grad, v_grad = call(
        unpack_kernel,
        "unpack",
        2,
        [VMEM],
        [(HBM, shape(q.shape)), (HBM, shape(q.shape)), (HBM, shape(k.shape)), (HBM, shape(k.shape))],
        [pltpu.VMEM(k.shape, BF), pltpu.VMEM(k.shape, BF)],
        2 * HEADS + 2,
    )(out)
    return (
        attn.reshape(queries.shape),
        q_grad.reshape(queries.shape),
        k_grad.reshape(key_states.shape),
        v_grad.reshape(value_vectors.shape),
    )


def solution(mesh):
    wide = P("dp", None, "ctx", None, None)
    return jax.shard_map(
        on_device,
        mesh=mesh,
        in_specs=(wide, wide, wide, wide, P("dp", None, "ctx", None)),
        out_specs=(wide, wide, wide, wide),
        check_vma=False,
    )
```
